32 devices in a mesh: tm: 4 (over y, x), rows: 4 (over z), clip: 2 (over core).
Axes of the slice: x: 2, y: 2, z: 4, core: 2. Of those that a mesh axis runs over, the one named last changes fastest.
Arguments:
- features: bfloat16 [8, 16, 8, 9984], P('clip', 'tm', 'rows'), may hold values from -6 to 6
- lengths: int32 [8], replicated, may hold values from 1 to 16, as said below
- stored_slot: int32 [8], replicated, may hold values from 0 to 7, each once
- owner_slot: int32 [8], replicated, may hold values from 0 to 7, each once
- gain_first: float32 [96], replicated, may hold values from 0.1 to 1.9
- conv_first: bfloat16 [3, 3, 3, 96, 96], replicated, may hold values from -0.125 to 0.125
- bias_first: float32 [96], replicated, may hold values from -3 to 3
- gain_second: float32 [96], replicated, may hold values from 0.1 to 1.9
- conv_second: bfloat16 [3, 3, 3, 96, 96], replicated, may hold values from -0.125 to 0.125
- bias_second: float32 [96], replicated, may hold values from -3 to 3
- reduce_conv_weight: bfloat16 [3, 3, 96, 96], replicated, may hold values from -0.21875 to 0.21875
- reduce_conv_bias: float32 [96], replicated, may hold values from -3 to 3
Outputs:
- encoded: bfloat16 [8, 16, 4, 4992], P('clip', 'tm', 'rows')
The draws below stay inside these ranges and needn't reach their ends.
Inputs may be any that keep to these rules, and one draw needn't show every extreme that they name: `lengths`: some clip has all 16 frames. `stored_slot`: each clip has its own storage slot. `owner_slot`: each clip has its own output slot.
All inputs are finite; a program needn't handle non-finite values.
Results may differ from the reference program's by a relative error of at most 0.0051.
Values may be sent and summed in bfloat16 or wider, within the bound.
No kernel may reach another device: no remote copies, remote signals or barrier semaphores. Data moves between devices by JAX's collectives and lax.ppermute only.
A program may use at most 64 MiB of HBM per device.

```python
import jax
import jax.numpy as jnp
from jax import lax

CHANNELS = 96
WIDTH = 104
FRAMES = 16
HEIGHT = 8
CLIPS = 8


def draw_lengths(key, part):
    first_key, second_key = jax.random.split(key)
    base_len = jax.random.randint(first_key, (CLIPS,), 1, FRAMES + 1)
    full_clip = jax.random.randint(second_key, (), 0, CLIPS)
    return jnp.where(jnp.arange(CLIPS) == full_clip, FRAMES, base_len).astype(jnp.int32)


def levels(key, shape, shards, low, top_value):
    def one(dim, shards_of):
        heights = jax.random.uniform(jax.random.fold_in(jax.random.fold_in(key, 6), dim), (shards_of,), jnp.float32, low / len(shards), top_value / len(shards))
        return jnp.repeat(jnp.exp(heights), shape[dim] // shards_of).reshape((-1,) + (1,) * (len(shape) - dim - 1))

    level = one(*shards[0])
    for cut in shards[1:]:
        level = level * one(*cut)
    return level


def normal_values(key, shape, scale, bound, cuts=(), kind=jnp.bfloat16):
    values = jax.random.normal(key, shape, jnp.float32) * scale
    if len(cuts) > 0:
        values = levels(key, shape, cuts, -0.22, 0.18) * values
    return jnp.clip(values, min=-bound, max=bound).astype(kind)


def setup_inputs(seed: int = 0) -> dict:
    splits = jax.random.split(jax.random.key(seed), 13)
    features = normal_values(splits[0], (CLIPS, FRAMES, HEIGHT, WIDTH * CHANNELS), 1.0, 6.0, ((0, 2), (1, 4), (2, 4)))
    lengths = draw_lengths(jax.random.fold_in(splits[12], 71), 0)
    stored_slot = jax.random.permutation(splits[2], CLIPS).astype(jnp.int32)
    owner_slot = jax.random.permutation(splits[3], CLIPS).astype(jnp.int32)
    gain_first = jnp.clip(1.0 + 0.18 * jax.random.normal(splits[4], (CHANNELS,), jnp.float32), 0.1, 1.9)
    conv_first = normal_values(splits[5], (3, 3, 3, CHANNELS, CHANNELS), (27 * CHANNELS) ** -0.5, 0.125)
    bias_first = normal_values(splits[6], (CHANNELS,), 0.5, 3.0, (), jnp.float32)
    gain_second = jnp.clip(1.0 + 0.18 * jax.random.normal(splits[7], (CHANNELS,), jnp.float32), 0.1, 1.9)
    conv_second = normal_values(splits[8], (3, 3, 3, CHANNELS, CHANNELS), (27 * CHANNELS) ** -0.5, 0.125)
    bias_second = normal_values(splits[9], (CHANNELS,), 0.5, 3.0, (), jnp.float32)
    reduce_conv_weight = normal_values(splits[10], (3, 3, CHANNELS, CHANNELS), (9 * CHANNELS) ** -0.5, 0.21875)
    reduce_conv_bias = normal_values(splits[11], (CHANNELS,), 0.5, 3.0, (), jnp.float32)
    return {"features": features, "lengths": lengths, "stored_slot": stored_slot, "owner_slot": owner_slot, "gain_first": gain_first, "conv_first": conv_first, "bias_first": bias_first, "gain_second": gain_second, "conv_second": conv_second, "bias_second": bias_second, "reduce_conv_weight": reduce_conv_weight, "reduce_conv_bias": reduce_conv_bias}


NORM_EPS = 1e-06

def norm_silu(values, gain_vec):
    scaled = values * lax.rsqrt(lax.optimization_barrier(jnp.mean(values * values, axis=-1, keepdims=True)) + NORM_EPS) * gain_vec
    return jax.nn.silu(scaled)

def conv_valid(grown_block, kernel_weight, bias_vector):
    frames = grown_block.shape[0] - 2
    band_rows = grown_block.shape[1] - 2
    columns = grown_block.shape[2]
    channels = grown_block.shape[3]
    outputs = kernel_weight.shape[4]
    padded = jnp.pad(grown_block, ((0, 0), (0, 0), (1, 1), (0, 0)))
    running_sum = jnp.zeros((frames * band_rows * columns, outputs), jnp.float32)
    for step_t in range(3):
        for step_h in range(3):
            window = padded[step_t:step_t + frames, step_h:step_h + band_rows]
            tap_stack = jnp.concatenate([window[:, :, step_w:step_w + columns] for step_w in range(3)], axis=-1)
            running_sum = running_sum + jnp.dot(tap_stack.reshape(-1, 3 * channels), kernel_weight[step_t, step_h].reshape(3 * channels, outputs), preferred_element_type=jnp.float32)
    return (running_sum + bias_vector).reshape(frames, band_rows, columns, outputs)

def spatial_reduce(padded_frames, kernel_weight, bias_vector):
    frames = padded_frames.shape[0]
    half_rows = (padded_frames.shape[1] - 1) // 2
    columns = padded_frames.shape[2]
    channels = padded_frames.shape[3]
    outputs = kernel_weight.shape[3]
    padded = jnp.pad(padded_frames, ((0, 0), (0, 0), (0, 1), (0, 0)))
    running_sum = jnp.zeros((frames * half_rows * (columns // 2), outputs), jnp.float32)
    for step_h in range(3):
        row_band = padded[:, step_h:step_h + 2 * half_rows - 1:2]
        tap_stack = jnp.concatenate([row_band[:, :, step_w:step_w + columns - 1:2] for step_w in range(3)], axis=-1)
        running_sum = running_sum + jnp.dot(tap_stack.reshape(-1, 3 * channels), kernel_weight[step_h].reshape(3 * channels, outputs), preferred_element_type=jnp.float32)
    return (running_sum + bias_vector).reshape(frames, half_rows, columns // 2, outputs)

def encode_clip(feature_map, length, gain_first, conv_first, bias_first, gain_second, conv_second, bias_second, reduce_conv_weight, reduce_conv_bias):
    first_act = norm_silu(feature_map.astype(jnp.float32), gain_first).astype(jnp.bfloat16)
    first_conv = conv_valid(jnp.pad(first_act, ((2, 0), (1, 1), (0, 0), (0, 0))), conv_first, bias_first)
    second_act = norm_silu(first_conv, gain_second).astype(jnp.bfloat16)
    branch = conv_valid(jnp.pad(second_act, ((2, 0), (1, 1), (0, 0), (0, 0))), conv_second, bias_second)
    residual_block_output = (feature_map.astype(jnp.float32) + branch).astype(jnp.bfloat16)
    spatial_reduced = spatial_reduce(jnp.pad(residual_block_output, ((0, 0), (0, 1), (0, 0), (0, 0))), reduce_conv_weight, reduce_conv_bias)
    alive_frame = jnp.arange(feature_map.shape[0], dtype=jnp.int32) < length
    return jnp.where(alive_frame[:, None, None, None], spatial_reduced, 0.0).astype(jnp.bfloat16)

def reference(features, lengths, stored_slot, owner_slot, gain_first, conv_first, bias_first, gain_second, conv_second, bias_second, reduce_conv_weight, reduce_conv_bias):

    def encode_one(clip_number):
        clip_data = features[stored_slot[clip_number]].reshape(FRAMES, HEIGHT, WIDTH, CHANNELS)
        result = encode_clip(clip_data, lengths[clip_number], gain_first, conv_first, bias_first, gain_second, conv_second, bias_second, reduce_conv_weight, reduce_conv_bias)
        return result.reshape(FRAMES, HEIGHT // 2, WIDTH // 2 * CHANNELS)
    results = lax.map(encode_one, jnp.arange(CLIPS, dtype=jnp.int32))
    inverse = jnp.zeros((CLIPS,), jnp.int32).at[owner_slot].set(jnp.arange(CLIPS, dtype=jnp.int32))
    return results[inverse]
```

```python
import functools

import jax
import jax.numpy as jnp
from jax import lax
from jax.experimental import pallas as pl
from jax.experimental.pallas import tpu as pltpu
from jax.sharding import PartitionSpec as P

NORM_EPS = 1e-06
LANES = 128
LEFT, RIGHT = 2, 4


def from_behind(value, axis, steps):
    count = lax.axis_size(axis)
    first, last = (max(0, -steps), min(count, count - steps))
    return lax.ppermute(value, axis, [(source, source + steps) for source in range(first, last)])


def padded_2(x, sides, width):
    for axis, dim in sides:
        count, length = (lax.axis_size(axis), x.shape[dim])
        up = [(i, (i + 1) % count) for i in range(count - 1)]
        down = [(j, i) for i, j in up]
        last = lax.slice_in_dim(x, length - width, length, axis=dim)
        first = lax.slice_in_dim(x, 0, width, axis=dim)
        before = lax.ppermute(last, axis, up)
        after = lax.ppermute(first, axis, down)
        x = jnp.concatenate([before, x, after], axis=dim)
    return x


def norm_silu(values, gain_vec):
    scaled = (
        values * lax.rsqrt(jnp.mean(values * values, axis=-1, keepdims=True) + NORM_EPS) * gain_vec
    )
    return jax.nn.silu(scaled)


def conv_valid(grown_block, kernel_weight, bias_vector):
    batch = grown_block.shape[0]
    frames = grown_block.shape[1] - 2
    band_rows = grown_block.shape[2] - 2
    columns = grown_block.shape[3]
    channels = grown_block.shape[4]
    outputs = kernel_weight.shape[4]
    padded = jnp.pad(grown_block, ((0, 0), (0, 0), (0, 0), (1, 1), (0, 0)))
    running_sum = jnp.zeros((batch * frames * band_rows * columns, outputs), jnp.float32)
    for step_t in range(3):
        for step_h in range(3):
            window = padded[:, step_t : step_t + frames, step_h : step_h + band_rows]
            tap_stack = jnp.concatenate(
                [window[:, :, :, step_w : step_w + columns] for step_w in range(3)], axis=-1
            )
            running_sum = running_sum + jnp.dot(
                tap_stack.reshape(-1, 3 * channels),
                kernel_weight[step_t, step_h].reshape(3 * channels, outputs),
                preferred_element_type=jnp.float32,
            )
    return (running_sum + bias_vector).reshape(batch, frames, band_rows, columns, outputs)


def spatial_reduce(padded_frames, kernel_weight, bias_vector):
    batch = padded_frames.shape[0]
    frames = padded_frames.shape[1]
    half_rows = (padded_frames.shape[2] - 1) // 2
    columns = padded_frames.shape[3]
    channels = padded_frames.shape[4]
    outputs = kernel_weight.shape[3]
    padded = jnp.pad(padded_frames, ((0, 0), (0, 0), (0, 0), (0, 1), (0, 0)))
    running_sum = jnp.zeros((batch * frames * half_rows * (columns // 2), outputs), jnp.float32)
    for step_h in range(3):
        row_band = padded[:, :, step_h : step_h + 2 * half_rows - 1 : 2]
        tap_stack = jnp.concatenate(
            [row_band[:, :, :, step_w : step_w + columns - 1 : 2] for step_w in range(3)], axis=-1
        )
        running_sum = running_sum + jnp.dot(
            tap_stack.reshape(-1, 3 * channels),
            kernel_weight[step_h].reshape(3 * channels, outputs),
            preferred_element_type=jnp.float32,
        )
    return (running_sum + bias_vector).reshape(batch, frames, half_rows, columns // 2, outputs)


def encode(
    clip_block,
    length,
    gain_first,
    conv_first,
    bias_first,
    gain_second,
    conv_second,
    bias_second,
    reduce_conv_weight,
    reduce_conv_bias,
):
    batch = clip_block.shape[0]
    frames = clip_block.shape[1]
    band_rows = clip_block.shape[2]
    channels = gain_first.shape[0]
    columns = clip_block.shape[3] // channels
    feature_map = clip_block.reshape(batch, frames, band_rows, columns, channels)
    first_frame = lax.axis_index("tm") * frames
    first_act = norm_silu(feature_map.astype(jnp.float32), gain_first).astype(jnp.bfloat16)
    earlier = from_behind(first_act[:, frames - 2 :], "tm", 1)
    grown_block = padded_2(jnp.concatenate([earlier, first_act], axis=1), (("rows", 2),), 1)
    first_conv = conv_valid(grown_block, conv_first, bias_first)
    second_act = norm_silu(first_conv, gain_second).astype(jnp.bfloat16)
    earlier_two = from_behind(second_act[:, frames - 2 :], "tm", 1)
    grown_two = padded_2(jnp.concatenate([earlier_two, second_act], axis=1), (("rows", 2),), 1)
    branch = conv_valid(grown_two, conv_second, bias_second)
    residual_block_output = (feature_map.astype(jnp.float32) + branch).astype(jnp.bfloat16)
    lower_neighbor_row = from_behind(residual_block_output[:, :, :1], "rows", -1)
    spatial_reduced = spatial_reduce(
        jnp.concatenate([residual_block_output, lower_neighbor_row], axis=2),
        reduce_conv_weight,
        reduce_conv_bias,
    )
    alive_frame = (first_frame + jnp.arange(frames, dtype=jnp.int32))[None, :] < length[:, None]
    masked = jnp.where(alive_frame[:, :, None, None, None], spatial_reduced, 0.0).astype(
        jnp.bfloat16
    )
    return masked.reshape(batch, frames, band_rows // 2, columns // 2 * channels)


def general_local(
    features,
    lengths,
    stored_slot,
    owner_slot,
    gain_first,
    conv_first,
    bias_first,
    gain_second,
    conv_second,
    bias_second,
    reduce_conv_weight,
    reduce_conv_bias,
):
    local_count = features.shape[0]
    my_slots = lax.axis_index("clip") * local_count + jnp.arange(local_count, dtype=jnp.int32)
    numbers = jnp.arange(stored_slot.shape[0], dtype=jnp.int32)
    placed = (stored_slot[:, None] == numbers[None, :]).astype(jnp.int32)
    target = jnp.sum(placed * owner_slot[:, None], axis=0)
    hits = (stored_slot[None, :] == my_slots[:, None]).astype(jnp.int32)
    length = jnp.sum(hits * lengths[None, :], axis=1)
    local_out = encode(
        features,
        length,
        gain_first,
        conv_first,
        bias_first,
        gain_second,
        conv_second,
        bias_second,
        reduce_conv_weight,
        reduce_conv_bias,
    )
    shard_piece = lax.all_gather(local_out, "clip", axis=0, tiled=True)
    sources = jnp.arange(shard_piece.shape[0], dtype=jnp.int32)
    source_hits = (sources[:, None] == numbers[None, :]).astype(jnp.int32)
    goes_to = jnp.sum(source_hits * target[None, :], axis=1)
    weights = (goes_to[None, :] == my_slots[:, None]).astype(shard_piece.dtype)
    return jnp.einsum(
        "ki,iabc->kabc", weights, shard_piece, preferred_element_type=jnp.float32
    ).astype(shard_piece.dtype)


class Plan:
    def __init__(self, mesh, features, channels):
        self.blocks, self.bands, self.cores = (mesh.shape[a] for a in ("tm", "rows", "clip"))
        self.clips = features.shape[0] // self.cores
        self.frames = features.shape[1] // self.blocks
        self.band = features.shape[2] // self.bands
        self.all_frames, self.height = features.shape[1], features.shape[2]
        self.channels = channels
        self.width = features.shape[3] // channels
        self.parts = self.blocks
        self.own = self.width // self.parts
        self.window = self.own + LEFT + RIGHT
        self.pairs = self.window // 2
        self.devices = self.blocks * self.bands

    def fits(self):
        return (
            self.bands == self.clips
            and self.width % (2 * self.parts) == 0
            and self.channels <= LANES
            and self.band == 2
            and self.band * self.frames == 8
            and self.all_frames == 16
            and (self.window * self.channels) % LANES == 0
        )


def lanes_of(shape):
    return lax.broadcasted_iota(jnp.int32, shape, len(shape) - 1)


def spread_columns(plan, dense, column):
    start = column * plan.channels
    first, off = start // LANES * LANES, start % LANES
    value = dense[:, first : first + LANES]
    if off + plan.channels > LANES:
        following = dense[:, first + LANES : first + 2 * LANES]
        value = jnp.where(lanes_of(value.shape) >= off, value, following)
    if off:
        value = pltpu.roll(value, LANES - off, 1)
    return jnp.where(lanes_of(value.shape) < plan.channels, value, 0.0)


def merge_columns(plan, columns):
    rows = columns[0].shape[0]
    total = -(-len(columns) * plan.channels // LANES)
    merged = [None] * total
    for index, value in enumerate(columns):
        start = index * plan.channels
        first, off = start // LANES, start % LANES
        turned = pltpu.roll(value, off, 1) if off else value
        lane = lanes_of((rows, LANES))
        merged[first] = turned if off == 0 else jnp.where(lane >= off, turned, merged[first])
        if off + plan.channels > LANES:
            merged[first + 1] = turned
    return merged


def encode_kernel(
    plan,
    lengths_ref,
    stored_ref,
    pieces_ref,
    gain_first_ref,
    weight_first_ref,
    bias_first_ref,
    gain_second_ref,
    weight_second_ref,
    bias_second_ref,
    weight_reduce_ref,
    bias_reduce_ref,
    out_ref,
    x_ref,
    act_ref,
    conv_ref,
    block_ref,
    big_ref,
    big_reduce_ref,
    vector_ref,
):
    frames, height, pairs, channels = plan.all_frames, plan.height, plan.pairs, plan.channels
    rows = height * frames
    part = lax.axis_index("tm")
    slot = lax.axis_index("clip") * plan.clips + lax.axis_index("rows")

    vector_ref[...] = jnp.zeros_like(vector_ref)
    for row, ref in enumerate(
        (gain_first_ref, bias_first_ref, gain_second_ref, bias_second_ref, bias_reduce_ref)
    ):
        vector_ref[row : row + 1, 0:channels] = ref[...]

    half = plan.frames
    sublane = lax.broadcasted_iota(jnp.int32, (8, LANES), 0)
    for band in range(plan.bands):
        dense = [
            pieces_ref[block * plan.bands + band].astype(jnp.float32)
            for block in range(plan.blocks)
        ]
        for column in range(plan.window):
            spread = [spread_columns(plan, piece, column) for piece in dense]
            turned = [pltpu.roll(value, half, 0) for value in spread]
            upper = [
                jnp.where(sublane < half, spread[2 * i], turned[2 * i + 1])
                for i in range(len(spread) // 2)
            ]
            lower = [
                jnp.where(sublane < half, turned[2 * i], spread[2 * i + 1])
                for i in range(len(spread) // 2)
            ]
            x_ref[column, 2 * band] = jnp.concatenate(upper, axis=0)
            x_ref[column, 2 * band + 1] = jnp.concatenate(lower, axis=0)

    def sum_matrix():
        shape = (2 * LANES, 2 * LANES)
        across = lax.broadcasted_iota(jnp.int32, shape, 0) // LANES
        along = lax.broadcasted_iota(jnp.int32, shape, 1) // LANES
        return jnp.where(across == along, 1.0, 0.0).astype(jnp.bfloat16)

    ones = sum_matrix()
    frame_of_row = lax.broadcasted_iota(jnp.int32, (rows, 2 * LANES), 0) % frames

    def in_image(pair):
        lane = lax.broadcasted_iota(jnp.int32, (1, 2 * LANES), 1)
        column = part * plan.own - LEFT + 2 * pair + lane // LANES
        return (column >= 0) & (column < plan.width)

    def activate(pair, values, gain):
        squares = (values * values).astype(jnp.bfloat16)
        sums = jnp.dot(squares, ones, preferred_element_type=jnp.float32)
        scale = jnp.where(in_image(pair), gain * (0.5 * channels**0.5), 0.0)
        scaled = values * lax.rsqrt(sums + channels * NORM_EPS) * scale
        act = scaled + scaled * jnp.tanh(scaled)
        for shift in range(3):
            moved = act
            if shift:
                moved = jnp.where(frame_of_row >= shift, pltpu.roll(act, shift, 0), 0.0)
            moved = moved.astype(jnp.bfloat16)
            for side in range(2):
                act_ref[2 - shift, 2 * pair + side + 1, 1 : height + 1] = moved[
                    :, side * LANES : (side + 1) * LANES
                ].reshape(height, frames, LANES)

    def both(row):
        vector = vector_ref[row : row + 1, :]
        return jnp.concatenate([vector, vector], axis=1)

    def spread_weights(weight_ref):
        big_ref[...] = jnp.zeros_like(big_ref)
        for tap in range(9):
            for side in range(2):
                for step in range(3):
                    first = (tap * 4 + side + step) * LANES
                    big_ref[
                        first : first + channels, side * LANES : side * LANES + channels
                    ] = weight_ref[tap * 3 + step]

    def convolve(first_pair, count):
        parts = []
        for tap in range(9):
            step_t, step_h = tap // 3, tap % 3
            for step in range(4):
                parts.append(
                    jnp.concatenate(
                        [
                            act_ref[
                                step_t, 2 * (first_pair + i) + step, step_h : step_h + height
                            ].reshape(rows, LANES)
                            for i in range(count)
                        ],
                        axis=0,
                    )
                )
        stack = jnp.concatenate(parts, axis=1)
        return jnp.dot(stack, big_ref[...], preferred_element_type=jnp.float32)

    act_ref[:, :, 0] = jnp.zeros_like(act_ref[:, :, 0])
    act_ref[:, :, height + 1] = jnp.zeros_like(act_ref[:, :, height + 1])
    act_ref[:, 0] = jnp.zeros_like(act_ref[:, 0])

    gain_first, gain_second = both(0), both(2)
    bias_first, bias_second = both(1), both(3)

    spread_weights(weight_first_ref)

    @pl.loop(0, pairs)
    def _(pair):
        values = jnp.concatenate(
            [x_ref[2 * pair + side].reshape(rows, LANES) for side in range(2)], axis=1
        )
        activate(pair, values, gain_first)

    group = 3

    @pl.loop(0, (pairs - 1) // group)
    def _(step):
        result = convolve(step * group, group) + bias_first
        for i in range(group):
            conv_ref[step * group + i] = result[i * rows : (i + 1) * rows]

    spread_weights(weight_second_ref)

    @pl.loop(0, pairs - 1)
    def _(pair):
        activate(pair, conv_ref[pair], gain_second)

    block_ref[:, height] = jnp.zeros_like(block_ref[:, height])
    pair_count = 2

    @pl.loop(0, (pairs - 2) // pair_count)
    def _(step):
        result = convolve(1 + step * pair_count, pair_count) + bias_second
        for i in range(pair_count):
            pair = 1 + step * pair_count + i
            for side in range(2):
                value = result[i * rows : (i + 1) * rows, side * LANES : (side + 1) * LANES]
                value = value.reshape(height, frames, LANES) + x_ref[2 * pair + side]
                column = part * plan.own - LEFT + 2 * pair + side
                value = jnp.where((column >= 0) & (column < plan.width), value, 0.0)
                block_ref[2 * pair + side, 0:height] = value.astype(jnp.bfloat16)

    big_reduce_ref[...] = jnp.zeros_like(big_reduce_ref)
    for tap in range(9):
        big_reduce_ref[tap * LANES : tap * LANES + channels, 0:channels] = weight_reduce_ref[tap]

    length = jnp.int32(0)
    for clip in range(lengths_ref.shape[0]):
        length = length + jnp.where(stored_ref[clip] == slot, lengths_ref[clip], 0)

    outputs, half_rows = plan.own // 2, height // 2
    columns = []
    for j in range(outputs):
        parts = []
        for tap in range(9):
            step_h, step_w = tap // 3, tap % 3
            parts.append(
                jnp.concatenate(
                    [block_ref[LEFT + 2 * j + step_w, 2 * i + step_h] for i in range(half_rows)],
                    axis=0,
                )
            )
        stack = jnp.concatenate(parts, axis=1)
        columns.append(stack)
    stack = jnp.concatenate(columns, axis=0)
    reduced = jnp.dot(stack, big_reduce_ref[...], preferred_element_type=jnp.float32)
    reduced = reduced + vector_ref[4:5, :]
    alive = lax.broadcasted_iota(jnp.int32, (half_rows * frames, LANES), 0) % frames < length
    size = half_rows * frames
    merged = merge_columns(
        plan, [jnp.where(alive, reduced[j * size : (j + 1) * size], 0.0) for j in range(outputs)]
    )
    for tile, value in enumerate(merged):
        for i in range(half_rows):
            for block in range(plan.blocks):
                first = i * frames + block * plan.frames
                out_ref[block * plan.bands + i, :, tile * LANES : (tile + 1) * LANES] = value[
                    first : first + plan.frames
                ].astype(jnp.bfloat16)


def encode_window(
    plan, pieces, lengths, stored_slot, gain_first, conv_first, bias_first, gain_second,
    conv_second, bias_second, reduce_conv_weight, reduce_conv_bias,
):
    channels, pairs = plan.channels, plan.pairs
    rows = plan.height * plan.all_frames
    out_tiles = -(-plan.own // 2 * channels // LANES)
    vmem = pl.BlockSpec(memory_space=pltpu.VMEM)
    smem = pl.BlockSpec(memory_space=pltpu.SMEM)
    return pl.pallas_call(
        functools.partial(encode_kernel, plan),
        out_shape=jax.ShapeDtypeStruct(
            (plan.devices, plan.frames, out_tiles * LANES), jnp.bfloat16
        ),
        in_specs=[smem, smem] + [vmem] * 9,
        out_specs=vmem,
        scratch_shapes=[
            pltpu.VMEM((plan.window, plan.height, plan.all_frames, LANES), jnp.float32),
            pltpu.VMEM((3, plan.window + 2, plan.height + 2, plan.all_frames, LANES), jnp.bfloat16),
            pltpu.VMEM((pairs, rows, 2 * LANES), jnp.float32),
            pltpu.VMEM((plan.window, plan.height + 1, plan.all_frames, LANES), jnp.bfloat16),
            pltpu.VMEM((9 * 4 * LANES, 2 * LANES), jnp.bfloat16),
            pltpu.VMEM((9 * LANES, LANES), jnp.bfloat16),
            pltpu.VMEM((8, LANES), jnp.float32),
        ],
        compiler_params=pltpu.CompilerParams(vmem_limit_bytes=48 * 2**20),
    )(
        lengths,
        stored_slot,
        pieces,
        gain_first.reshape(1, channels),
        conv_first.reshape(27, channels, channels),
        bias_first.reshape(1, channels),
        gain_second.reshape(1, channels),
        conv_second.reshape(27, channels, channels),
        bias_second.reshape(1, channels),
        reduce_conv_weight.reshape(9, channels, channels),
        reduce_conv_bias.reshape(1, channels),
    )


def window_local(
    plan, features, lengths, stored_slot, owner_slot, gain_first, conv_first, bias_first,
    gain_second, conv_second, bias_second, reduce_conv_weight, reduce_conv_bias,
):
    channels, clips, parts = plan.channels, plan.clips, plan.parts
    piece_rows = plan.frames * plan.band
    dense = features.transpose(0, 2, 1, 3).reshape(clips, piece_rows, -1)
    dense = jnp.pad(dense, ((0, 0), (0, 0), (LEFT * channels, RIGHT * channels)))
    pieces = jnp.concatenate(
        [
            dense[:, :, q * plan.own * channels :][:, :, : plan.window * channels]
            for q in range(parts)
        ],
        axis=0,
    )
    pieces = lax.all_to_all(pieces, ("tm", "rows"), 0, 0, tiled=True)
    out = encode_window(
        plan, pieces, lengths, stored_slot, gain_first, conv_first, bias_first, gain_second,
        conv_second, bias_second, reduce_conv_weight, reduce_conv_bias,
    )
    out = lax.all_to_all(out, ("tm", "rows"), 0, 0, tiled=True)
    used = plan.own // 2 * channels
    out = out[:, :, :used].reshape(parts, clips, plan.frames, used)
    out = out.transpose(1, 2, 0, 3).reshape(clips, plan.frames, 1, parts * used)
    both = lax.all_gather(out, "clip", axis=0, tiled=True)
    numbers = jnp.arange(stored_slot.shape[0], dtype=jnp.int32)
    my_slots = lax.axis_index("clip") * clips + numbers[:clips]
    wanted = (owner_slot[None, :] == my_slots[:, None]).astype(jnp.int32)
    source = jnp.sum(wanted * stored_slot[None, :], axis=1)
    weights = (source[:, None] == numbers[None, :]).astype(out.dtype)
    return jnp.einsum(
        "ki,iabc->kabc", weights, both, preferred_element_type=jnp.float32
    ).astype(out.dtype)


def solution(mesh):
    out_specs = P("clip", "tm", "rows", None)
    in_specs = (out_specs,) + (P(),) * 11

    def run(features, *others):
        plan = Plan(mesh, features, others[3].shape[0])
        inner = functools.partial(window_local, plan) if plan.fits() else general_local
        return jax.shard_map(
            inner, mesh=mesh, in_specs=in_specs, out_specs=out_specs, check_vma=False
        )(features, *others)

    return run
```

```python
import functools

import jax
import jax.numpy as jnp
from jax import lax
from jax.experimental import pallas as pl
from jax.experimental.pallas import tpu as pltpu
from jax.sharding import PartitionSpec as P

NORM_EPS = 1e-06
LANES = 128
LEFT, RIGHT = 2, 4


def from_behind(value, axis, steps):
    count = lax.axis_size(axis)
    first, last = (max(0, -steps), min(count, count - steps))
    return lax.ppermute(value, axis, [(source, source + steps) for source in range(first, last)])


def padded_2(x, sides, width):
    for axis, dim in sides:
        count, length = (lax.axis_size(axis), x.shape[dim])
        up = [(i, (i + 1) % count) for i in range(count - 1)]
        down = [(j, i) for i, j in up]
        last = lax.slice_in_dim(x, length - width, length, axis=dim)
        first = lax.slice_in_dim(x, 0, width, axis=dim)
        before = lax.ppermute(last, axis, up)
        after = lax.ppermute(first, axis, down)
        x = jnp.concatenate([before, x, after], axis=dim)
    return x


def norm_silu(values, gain_vec):
    scaled = (
        values * lax.rsqrt(jnp.mean(values * values, axis=-1, keepdims=True) + NORM_EPS) * gain_vec
    )
    return jax.nn.silu(scaled)


def conv_valid(grown_block, kernel_weight, bias_vector):
    batch = grown_block.shape[0]
    frames = grown_block.shape[1] - 2
    band_rows = grown_block.shape[2] - 2
    columns = grown_block.shape[3]
    channels = grown_block.shape[4]
    outputs = kernel_weight.shape[4]
    padded = jnp.pad(grown_block, ((0, 0), (0, 0), (0, 0), (1, 1), (0, 0)))
    running_sum = jnp.zeros((batch * frames * band_rows * columns, outputs), jnp.float32)
    for step_t in range(3):
        for step_h in range(3):
            window = padded[:, step_t : step_t + frames, step_h : step_h + band_rows]
            tap_stack = jnp.concatenate(
                [window[:, :, :, step_w : step_w + columns] for step_w in range(3)], axis=-1
            )
            running_sum = running_sum + jnp.dot(
                tap_stack.reshape(-1, 3 * channels),
                kernel_weight[step_t, step_h].reshape(3 * channels, outputs),
                preferred_element_type=jnp.float32,
            )
    return (running_sum + bias_vector).reshape(batch, frames, band_rows, columns, outputs)


def spatial_reduce(padded_frames, kernel_weight, bias_vector):
    batch = padded_frames.shape[0]
    frames = padded_frames.shape[1]
    half_rows = (padded_frames.shape[2] - 1) // 2
    columns = padded_frames.shape[3]
    channels = padded_frames.shape[4]
    outputs = kernel_weight.shape[3]
    padded = jnp.pad(padded_frames, ((0, 0), (0, 0), (0, 0), (0, 1), (0, 0)))
    running_sum = jnp.zeros((batch * frames * half_rows * (columns // 2), outputs), jnp.float32)
    for step_h in range(3):
        row_band = padded[:, :, step_h : step_h + 2 * half_rows - 1 : 2]
        tap_stack = jnp.concatenate(
            [row_band[:, :, :, step_w : step_w + columns - 1 : 2] for step_w in range(3)], axis=-1
        )
        running_sum = running_sum + jnp.dot(
            tap_stack.reshape(-1, 3 * channels),
            kernel_weight[step_h].reshape(3 * channels, outputs),
            preferred_element_type=jnp.float32,
        )
    return (running_sum + bias_vector).reshape(batch, frames, half_rows, columns // 2, outputs)


def encode(
    clip_block,
    length,
    gain_first,
    conv_first,
    bias_first,
    gain_second,
    conv_second,
    bias_second,
    reduce_conv_weight,
    reduce_conv_bias,
):
    batch = clip_block.shape[0]
    frames = clip_block.shape[1]
    band_rows = clip_block.shape[2]
    channels = gain_first.shape[0]
    columns = clip_block.shape[3] // channels
    feature_map = clip_block.reshape(batch, frames, band_rows, columns, channels)
    first_frame = lax.axis_index("tm") * frames
    first_act = norm_silu(feature_map.astype(jnp.float32), gain_first).astype(jnp.bfloat16)
    earlier = from_behind(first_act[:, frames - 2 :], "tm", 1)
    grown_block = padded_2(jnp.concatenate([earlier, first_act], axis=1), (("rows", 2),), 1)
    first_conv = conv_valid(grown_block, conv_first, bias_first)
    second_act = norm_silu(first_conv, gain_second).astype(jnp.bfloat16)
    earlier_two = from_behind(second_act[:, frames - 2 :], "tm", 1)
    grown_two = padded_2(jnp.concatenate([earlier_two, second_act], axis=1), (("rows", 2),), 1)
    branch = conv_valid(grown_two, conv_second, bias_second)
    residual_block_output = (feature_map.astype(jnp.float32) + branch).astype(jnp.bfloat16)
    lower_neighbor_row = from_behind(residual_block_output[:, :, :1], "rows", -1)
    spatial_reduced = spatial_reduce(
        jnp.concatenate([residual_block_output, lower_neighbor_row], axis=2),
        reduce_conv_weight,
        reduce_conv_bias,
    )
    alive_frame = (first_frame + jnp.arange(frames, dtype=jnp.int32))[None, :] < length[:, None]
    masked = jnp.where(alive_frame[:, :, None, None, None], spatial_reduced, 0.0).astype(
        jnp.bfloat16
    )
    return masked.reshape(batch, frames, band_rows // 2, columns // 2 * channels)


def general_local(
    features,
    lengths,
    stored_slot,
    owner_slot,
    gain_first,
    conv_first,
    bias_first,
    gain_second,
    conv_second,
    bias_second,
    reduce_conv_weight,
    reduce_conv_bias,
):
    local_count = features.shape[0]
    my_slots = lax.axis_index("clip") * local_count + jnp.arange(local_count, dtype=jnp.int32)
    numbers = jnp.arange(stored_slot.shape[0], dtype=jnp.int32)
    placed = (stored_slot[:, None] == numbers[None, :]).astype(jnp.int32)
    target = jnp.sum(placed * owner_slot[:, None], axis=0)
    hits = (stored_slot[None, :] == my_slots[:, None]).astype(jnp.int32)
    length = jnp.sum(hits * lengths[None, :], axis=1)
    local_out = encode(
        features,
        length,
        gain_first,
        conv_first,
        bias_first,
        gain_second,
        conv_second,
        bias_second,
        reduce_conv_weight,
        reduce_conv_bias,
    )
    shard_piece = lax.all_gather(local_out, "clip", axis=0, tiled=True)
    sources = jnp.arange(shard_piece.shape[0], dtype=jnp.int32)
    source_hits = (sources[:, None] == numbers[None, :]).astype(jnp.int32)
    goes_to = jnp.sum(source_hits * target[None, :], axis=1)
    weights = (goes_to[None, :] == my_slots[:, None]).astype(shard_piece.dtype)
    return jnp.einsum(
        "ki,iabc->kabc", weights, shard_piece, preferred_element_type=jnp.float32
    ).astype(shard_piece.dtype)


CHUNKS = 4


class Plan:
    def __init__(self, mesh, features, channels):
        self.blocks, self.bands, self.cores = (mesh.shape[a] for a in ("tm", "rows", "clip"))
        self.clips = features.shape[0] // self.cores
        self.frames = features.shape[1] // self.blocks
        self.band = features.shape[2] // self.bands
        self.all_frames, self.height = features.shape[1], features.shape[2]
        self.channels = channels
        self.width = features.shape[3] // channels
        self.parts = self.blocks
        self.own = self.width // self.parts
        self.window = self.own + LEFT + RIGHT
        self.pairs = self.window // 2
        self.devices = self.blocks * self.bands

    def fits(self):
        return (
            self.bands == self.clips
            and self.width % (2 * self.parts) == 0
            and 3 * (LANES - self.channels) == self.channels
            and self.band == 2
            and self.band * self.frames == 8
            and self.all_frames == 16
            and (self.window * self.channels) % LANES == 0
        )


def lanes_of(shape):
    return lax.broadcasted_iota(jnp.int32, shape, len(shape) - 1)


def spread_columns(plan, dense, column):
    start = column * plan.channels
    first, off = start // LANES * LANES, start % LANES
    value = dense[:, first : first + LANES]
    if off + plan.channels > LANES:
        following = dense[:, first + LANES : first + 2 * LANES]
        value = jnp.where(lanes_of(value.shape) >= off, value, following)
    if off:
        value = pltpu.roll(value, LANES - off, 1)
    return jnp.where(lanes_of(value.shape) < plan.channels, value, 0.0)


def merge_columns(plan, columns):
    rows = columns[0].shape[0]
    total = -(-len(columns) * plan.channels // LANES)
    merged = [None] * total
    for index, value in enumerate(columns):
        start = index * plan.channels
        first, off = start // LANES, start % LANES
        turned = pltpu.roll(value, off, 1) if off else value
        lane = lanes_of((rows, LANES))
        merged[first] = turned if off == 0 else jnp.where(lane >= off, turned, merged[first])
        if off + plan.channels > LANES:
            merged[first + 1] = turned
    return merged


def weights_kernel(plan, first_ref, second_ref, reduce_ref, big_first_ref, big_second_ref, big_reduce_ref):
    channels = plan.channels
    spare = LANES - channels
    for weight_ref, big_ref in ((first_ref, big_first_ref), (second_ref, big_second_ref)):
        big_ref[...] = jnp.zeros_like(big_ref)
        for tap in range(9):
            for side in range(2):
                for step in range(3):
                    tile = side + step
                    along = pl.ds(side * LANES, channels)
                    if tile < 3:
                        first = (tap * 3 + tile) * LANES
                        big_ref[first : first + channels, along] = weight_ref[tap * 3 + step]
                        continue
                    for tile in range(3):
                        first = (tap * 3 + tile) * LANES + channels
                        big_ref[first : first + spare, along] = weight_ref[
                            tap * 3 + step, tile * spare : (tile + 1) * spare
                        ]
    big_reduce_ref[...] = jnp.zeros_like(big_reduce_ref)
    for tap in range(9):
        big_reduce_ref[tap * LANES : tap * LANES + channels, 0:channels] = reduce_ref[tap]


def spread_weights(plan, conv_first, conv_second, reduce_conv_weight):
    channels = plan.channels
    vmem = pl.BlockSpec(memory_space=pltpu.VMEM)
    conv = jax.ShapeDtypeStruct((9 * 3 * LANES, 2 * LANES), jnp.bfloat16)
    reduction = jax.ShapeDtypeStruct((9 * LANES, LANES), jnp.bfloat16)
    return pl.pallas_call(
        functools.partial(weights_kernel, plan),
        out_shape=(conv, conv, reduction),
        in_specs=[vmem] * 3,
        out_specs=(vmem,) * 3,
        compiler_params=pltpu.CompilerParams(vmem_limit_bytes=16 * 2**20),
        cost_estimate=pl.CostEstimate(flops=0, transcendentals=0, bytes_accessed=6 * 2**20),
    )(
        conv_first.reshape(27, channels, channels),
        conv_second.reshape(27, channels, channels),
        reduce_conv_weight.reshape(9, channels, channels),
    )


def encode_kernel(
    plan,
    lengths_ref,
    stored_ref,
    pieces_ref,
    gain_first_ref,
    big_first_ref,
    bias_first_ref,
    gain_second_ref,
    big_second_ref,
    bias_second_ref,
    big_reduce_ref,
    bias_reduce_ref,
    out_ref,
    x_ref,
    act_first_ref,
    act_second_ref,
    wide_first_ref,
    wide_second_ref,
    conv_ref,
    block_ref,
    reduced_ref,
    vector_ref,
):
    frames, height, pairs, channels = plan.all_frames, plan.height, plan.pairs, plan.channels
    rows = height * frames
    part = lax.axis_index("tm")
    slot = lax.axis_index("clip") * plan.clips + lax.axis_index("rows")

    vector_ref[...] = jnp.zeros_like(vector_ref)
    for row, ref in enumerate(
        (gain_first_ref, bias_first_ref, gain_second_ref, bias_second_ref, bias_reduce_ref)
    ):
        vector_ref[row : row + 1, 0:channels] = ref[...]

    half = plan.frames
    sublane = lax.broadcasted_iota(jnp.int32, (8, LANES), 0)
    for band in range(plan.bands):
        dense = [
            pieces_ref[block * plan.bands + band].astype(jnp.float32)
            for block in range(plan.blocks)
        ]
        for column in range(plan.window):
            spread = [spread_columns(plan, piece, column) for piece in dense]
            turned = [pltpu.roll(value, half, 0) for value in spread]
            upper = [
                jnp.where(sublane < half, spread[2 * i], turned[2 * i + 1])
                for i in range(len(spread) // 2)
            ]
            lower = [
                jnp.where(sublane < half, turned[2 * i], spread[2 * i + 1])
                for i in range(len(spread) // 2)
            ]
            x_ref[column, 2 * band] = jnp.concatenate(upper, axis=0)
            x_ref[column, 2 * band + 1] = jnp.concatenate(lower, axis=0)

    def sum_matrix():
        shape = (2 * LANES, 2 * LANES)
        across = lax.broadcasted_iota(jnp.int32, shape, 0) // LANES
        along = lax.broadcasted_iota(jnp.int32, shape, 1) // LANES
        return jnp.where(across == along, 1.0, 0.0).astype(jnp.bfloat16)

    ones = sum_matrix()
    frame_of_row = lax.broadcasted_iota(jnp.int32, (rows, LANES), 0) % frames

    def in_image(pair):
        lane = lax.broadcasted_iota(jnp.int32, (1, 2 * LANES), 1)
        column = part * plan.own - LEFT + 2 * pair + lane // LANES
        return (column >= 0) & (column < plan.width)

    def activate(wide_ref, pair, values, gain):
        squares = (values * values).astype(jnp.bfloat16)
        sums = jnp.dot(squares, ones, preferred_element_type=jnp.float32)
        scale = jnp.where(in_image(pair), gain * (0.5 * channels**0.5), 0.0)
        scaled = values * lax.rsqrt(sums + channels * NORM_EPS) * scale
        wide_ref[pair + 1] = scaled + scaled * jnp.tanh(scaled)

    lane = lax.broadcasted_iota(jnp.int32, (rows, LANES), 1)

    def stack_window(wide_ref, act_ref, pair):
        before, after = wide_ref[pair, :, LANES:], wide_ref[pair + 2, :, :LANES]
        for tile, value in enumerate(
            (before, wide_ref[pair + 1, :, :LANES], wide_ref[pair + 1, :, LANES:])
        ):
            spill = pltpu.roll(after, channels - tile * (LANES - channels), 1)
            value = jnp.where(lane < channels, value, spill)
            for shift in range(3):
                moved = value
                if shift:
                    moved = jnp.where(frame_of_row >= shift, pltpu.roll(value, shift, 0), 0.0)
                act_ref[
                    2 - shift, pair, 1 : height + 1, :, tile * LANES : (tile + 1) * LANES
                ] = moved.astype(jnp.bfloat16).reshape(height, frames, LANES)

    def both(row):
        vector = vector_ref[row : row + 1, :]
        return jnp.concatenate([vector, vector], axis=1)

    def convolve(act_ref, big_ref, first_pair, count):
        parts = [
            act_ref[
                tap // 3, first_pair : first_pair + count, tap % 3 : tap % 3 + height
            ].reshape(
                count * rows, 3 * LANES
            )
            for tap in range(9)
        ]
        stack = jnp.concatenate(parts, axis=1)
        return jnp.dot(stack, big_ref[...], preferred_element_type=jnp.float32)

    for act_ref in (act_first_ref, act_second_ref):
        act_ref[:, :, 0] = jnp.zeros_like(act_ref[:, :, 0])
        act_ref[:, :, height + 1] = jnp.zeros_like(act_ref[:, :, height + 1])
    wide_first_ref[0] = jnp.zeros_like(wide_first_ref[0])
    wide_second_ref[pairs] = jnp.zeros_like(wide_second_ref[pairs])
    block_ref[:, height] = jnp.zeros_like(block_ref[:, height])

    gain_first, gain_second = both(0), both(2)
    bias_first, bias_second = both(1), both(3)

    def first_window(acts, windows):
        for pair in acts:
            values = jnp.concatenate(
                [x_ref[2 * pair + side].reshape(rows, LANES) for side in range(2)], axis=1
            )
            activate(wide_first_ref, pair, values, gain_first)
        for pair in windows:
            stack_window(wide_first_ref, act_first_ref, pair)

    def second_window(acts, windows):
        for pair in acts:
            activate(wide_second_ref, pair, conv_ref[pair], gain_second)
        for pair in windows:
            stack_window(wide_second_ref, act_second_ref, pair)

    def first_conv(todo):
        result = convolve(act_first_ref, big_first_ref, todo[0], len(todo)) + bias_first
        for i, pair in enumerate(todo):
            conv_ref[pair] = result[i * rows : (i + 1) * rows]

    def second_conv(todo):
        result = convolve(act_second_ref, big_second_ref, todo[0], len(todo)) + bias_second
        for i, pair in enumerate(todo):
            for side in range(2):
                value = result[i * rows : (i + 1) * rows, side * LANES : (side + 1) * LANES]
                value = value.reshape(height, frames, LANES) + x_ref[2 * pair + side]
                column = part * plan.own - LEFT + 2 * pair + side
                value = jnp.where((column >= 0) & (column < plan.width), value, 0.0)
                block_ref[2 * pair + side, 0:height] = value.astype(jnp.bfloat16)

    outputs, half_rows = plan.own // 2, height // 2
    size = half_rows * frames

    def reduce_conv(todo):
        stacks = [
            jnp.concatenate(
                [
                    jnp.concatenate(
                        [
                            block_ref[LEFT + 2 * j + tap % 3, 2 * i + tap // 3]
                            for i in range(half_rows)
                        ],
                        axis=0,
                    )
                    for tap in range(9)
                ],
                axis=1,
            )
            for j in todo
        ]
        result = jnp.dot(
            jnp.concatenate(stacks, axis=0),
            big_reduce_ref[...],
            preferred_element_type=jnp.float32,
        )
        for i, j in enumerate(todo):
            reduced_ref[j] = result[i * size : (i + 1) * size] + vector_ref[4:5, :]

    last = pairs - 1
    cuts = [0] + [last * (i + 1) // CHUNKS for i in range(CHUNKS)]
    first_chunks = [range(a, b) for a, b in zip(cuts[:-1], cuts[1:])]
    second_cuts = [1] + [cut - 1 for cut in cuts[1:-1]] + [last]
    second_chunks = [range(a, b) for a, b in zip(second_cuts[:-1], second_cuts[1:])]
    done = 0
    reduced_until = 0
    for step in range(CHUNKS + 4):
        if 0 <= step - 1 < CHUNKS:
            first_conv(first_chunks[step - 1])
        if 0 <= step - 3 < CHUNKS and len(second_chunks[step - 3]):
            second_conv(second_chunks[step - 3])
        if 0 <= step - 4 < CHUNKS:
            until = min(second_chunks[step - 4].stop - 2, outputs)
            if until > reduced_until:
                reduce_conv(range(reduced_until, until))
                reduced_until = until
        if step < CHUNKS:
            until = first_chunks[step].stop + 1
            first_window(range(done, until), first_chunks[step])
            done = until
        if 0 <= step - 2 < CHUNKS:
            second_window(first_chunks[step - 2], second_chunks[step - 2])

    length = jnp.int32(0)
    for clip in range(lengths_ref.shape[0]):
        length = length + jnp.where(stored_ref[clip] == slot, lengths_ref[clip], 0)

    alive = lax.broadcasted_iota(jnp.int32, (half_rows * frames, LANES), 0) % frames < length
    merged = merge_columns(
        plan, [jnp.where(alive, reduced_ref[j], 0.0) for j in range(outputs)]
    )
    for tile, value in enumerate(merged):
        for i in range(half_rows):
            for block in range(plan.blocks):
                first = i * frames + block * plan.frames
                out_ref[block * plan.bands + i, :, tile * LANES : (tile + 1) * LANES] = value[
                    first : first + plan.frames
                ].astype(jnp.bfloat16)


def encode_window(
    plan, pieces, lengths, stored_slot, gain_first, conv_first, bias_first, gain_second,
    conv_second, bias_second, reduce_conv_weight, reduce_conv_bias,
):
    channels, pairs = plan.channels, plan.pairs
    rows = plan.height * plan.all_frames
    out_tiles = -(-plan.own // 2 * channels // LANES)
    vmem = pl.BlockSpec(memory_space=pltpu.VMEM)
    smem = pl.BlockSpec(memory_space=pltpu.SMEM)
    return pl.pallas_call(
        functools.partial(encode_kernel, plan),
        out_shape=jax.ShapeDtypeStruct(
            (plan.devices, plan.frames, out_tiles * LANES), jnp.bfloat16
        ),
        in_specs=[smem, smem] + [vmem] * 9,
        out_specs=vmem,
        scratch_shapes=[
            pltpu.VMEM((plan.window, plan.height, plan.all_frames, LANES), jnp.float32),
            pltpu.VMEM((3, pairs, plan.height + 2, plan.all_frames, 3 * LANES), jnp.bfloat16),
            pltpu.VMEM((3, pairs, plan.height + 2, plan.all_frames, 3 * LANES), jnp.bfloat16),
            pltpu.VMEM((pairs + 2, rows, 2 * LANES), jnp.float32),
            pltpu.VMEM((pairs + 2, rows, 2 * LANES), jnp.float32),
            pltpu.VMEM((pairs, rows, 2 * LANES), jnp.float32),
            pltpu.VMEM((plan.window, plan.height + 1, plan.all_frames, LANES), jnp.bfloat16),
            pltpu.VMEM((plan.own // 2, rows // 2, LANES), jnp.float32),
            pltpu.VMEM((8, LANES), jnp.float32),
        ],
        compiler_params=pltpu.CompilerParams(vmem_limit_bytes=26 * 2**20),
    )(
        lengths,
        stored_slot,
        pieces,
        gain_first.reshape(1, channels),
        conv_first,
        bias_first.reshape(1, channels),
        gain_second.reshape(1, channels),
        conv_second,
        bias_second.reshape(1, channels),
        reduce_conv_weight,
        reduce_conv_bias.reshape(1, channels),
    )


def window_local(
    plan, features, lengths, stored_slot, owner_slot, gain_first, conv_first, bias_first,
    gain_second, conv_second, bias_second, reduce_conv_weight, reduce_conv_bias,
):
    channels, clips, parts = plan.channels, plan.clips, plan.parts
    piece_rows = plan.frames * plan.band
    dense = features.transpose(0, 2, 1, 3).reshape(clips, piece_rows, -1)
    dense = jnp.pad(dense, ((0, 0), (0, 0), (LEFT * channels, RIGHT * channels)))
    pieces = jnp.concatenate(
        [
            dense[:, :, q * plan.own * channels :][:, :, : plan.window * channels]
            for q in range(parts)
        ],
        axis=0,
    )
    conv_first, conv_second, reduce_conv_weight = spread_weights(
        plan, conv_first, conv_second, reduce_conv_weight
    )
    pieces = lax.all_to_all(pieces, ("tm", "rows"), 0, 0, tiled=True)
    out = encode_window(
        plan, pieces, lengths, stored_slot, gain_first, conv_first, bias_first, gain_second,
        conv_second, bias_second, reduce_conv_weight, reduce_conv_bias,
    )
    out = lax.all_to_all(out, ("tm", "rows"), 0, 0, tiled=True)
    used = plan.own // 2 * channels
    out = out[:, :, :used].reshape(parts, clips, plan.frames, used)
    out = out.transpose(1, 2, 0, 3).reshape(clips, plan.frames, 1, parts * used)
    both = lax.all_gather(out, "clip", axis=0, tiled=True)
    numbers = jnp.arange(stored_slot.shape[0], dtype=jnp.int32)
    my_slots = lax.axis_index("clip") * clips + numbers[:clips]
    wanted = (owner_slot[None, :] == my_slots[:, None]).astype(jnp.int32)
    source = jnp.sum(wanted * stored_slot[None, :], axis=1)
    weights = (source[:, None] == numbers[None, :]).astype(out.dtype)
    return jnp.einsum(
        "ki,iabc->kabc", weights, both, preferred_element_type=jnp.float32
    ).astype(out.dtype)


def solution(mesh):
    out_specs = P("clip", "tm", "rows", None)
    in_specs = (out_specs,) + (P(),) * 11

    def run(features, *others):
        plan = Plan(mesh, features, others[3].shape[0])
        inner = functools.partial(window_local, plan) if plan.fits() else general_local
        return jax.shard_map(
            inner, mesh=mesh, in_specs=in_specs, out_specs=out_specs, check_vma=False
        )(features, *others)

    return run
```

```python
import functools

import jax
import jax.numpy as jnp
from jax import lax
from jax.experimental import pallas as pl
from jax.experimental.pallas import tpu as pltpu
from jax.sharding import PartitionSpec as P

NORM_EPS = 1e-06
LANES = 128
LEFT, RIGHT = 2, 4


def from_behind(value, axis, steps):
    count = lax.axis_size(axis)
    first, last = (max(0, -steps), min(count, count - steps))
    return lax.ppermute(value, axis, [(source, source + steps) for source in range(first, last)])


def padded_2(x, sides, width):
    for axis, dim in sides:
        count, length = (lax.axis_size(axis), x.shape[dim])
        up = [(i, (i + 1) % count) for i in range(count - 1)]
        down = [(j, i) for i, j in up]
        last = lax.slice_in_dim(x, length - width, length, axis=dim)
        first = lax.slice_in_dim(x, 0, width, axis=dim)
        before = lax.ppermute(last, axis, up)
        after = lax.ppermute(first, axis, down)
        x = jnp.concatenate([before, x, after], axis=dim)
    return x


def norm_silu(values, gain_vec):
    scaled = (
        values * lax.rsqrt(jnp.mean(values * values, axis=-1, keepdims=True) + NORM_EPS) * gain_vec
    )
    return jax.nn.silu(scaled)


def conv_valid(grown_block, kernel_weight, bias_vector):
    batch = grown_block.shape[0]
    frames = grown_block.shape[1] - 2
    band_rows = grown_block.shape[2] - 2
    columns = grown_block.shape[3]
    channels = grown_block.shape[4]
    outputs = kernel_weight.shape[4]
    padded = jnp.pad(grown_block, ((0, 0), (0, 0), (0, 0), (1, 1), (0, 0)))
    running_sum = jnp.zeros((batch * frames * band_rows * columns, outputs), jnp.float32)
    for step_t in range(3):
        for step_h in range(3):
            window = padded[:, step_t : step_t + frames, step_h : step_h + band_rows]
            tap_stack = jnp.concatenate(
                [window[:, :, :, step_w : step_w + columns] for step_w in range(3)], axis=-1
            )
            running_sum = running_sum + jnp.dot(
                tap_stack.reshape(-1, 3 * channels),
                kernel_weight[step_t, step_h].reshape(3 * channels, outputs),
                preferred_element_type=jnp.float32,
            )
    return (running_sum + bias_vector).reshape(batch, frames, band_rows, columns, outputs)


def spatial_reduce(padded_frames, kernel_weight, bias_vector):
    batch = padded_frames.shape[0]
    frames = padded_frames.shape[1]
    half_rows = (padded_frames.shape[2] - 1) // 2
    columns = padded_frames.shape[3]
    channels = padded_frames.shape[4]
    outputs = kernel_weight.shape[3]
    padded = jnp.pad(padded_frames, ((0, 0), (0, 0), (0, 0), (0, 1), (0, 0)))
    running_sum = jnp.zeros((batch * frames * half_rows * (columns // 2), outputs), jnp.float32)
    for step_h in range(3):
        row_band = padded[:, :, step_h : step_h + 2 * half_rows - 1 : 2]
        tap_stack = jnp.concatenate(
            [row_band[:, :, :, step_w : step_w + columns - 1 : 2] for step_w in range(3)], axis=-1
        )
        running_sum = running_sum + jnp.dot(
            tap_stack.reshape(-1, 3 * channels),
            kernel_weight[step_h].reshape(3 * channels, outputs),
            preferred_element_type=jnp.float32,
        )
    return (running_sum + bias_vector).reshape(batch, frames, half_rows, columns // 2, outputs)


def encode(
    clip_block,
    length,
    gain_first,
    conv_first,
    bias_first,
    gain_second,
    conv_second,
    bias_second,
    reduce_conv_weight,
    reduce_conv_bias,
):
    batch = clip_block.shape[0]
    frames = clip_block.shape[1]
    band_rows = clip_block.shape[2]
    channels = gain_first.shape[0]
    columns = clip_block.shape[3] // channels
    feature_map = clip_block.reshape(batch, frames, band_rows, columns, channels)
    first_frame = lax.axis_index("tm") * frames
    first_act = norm_silu(feature_map.astype(jnp.float32), gain_first).astype(jnp.bfloat16)
    earlier = from_behind(first_act[:, frames - 2 :], "tm", 1)
    grown_block = padded_2(jnp.concatenate([earlier, first_act], axis=1), (("rows", 2),), 1)
    first_conv = conv_valid(grown_block, conv_first, bias_first)
    second_act = norm_silu(first_conv, gain_second).astype(jnp.bfloat16)
    earlier_two = from_behind(second_act[:, frames - 2 :], "tm", 1)
    grown_two = padded_2(jnp.concatenate([earlier_two, second_act], axis=1), (("rows", 2),), 1)
    branch = conv_valid(grown_two, conv_second, bias_second)
    residual_block_output = (feature_map.astype(jnp.float32) + branch).astype(jnp.bfloat16)
    lower_neighbor_row = from_behind(residual_block_output[:, :, :1], "rows", -1)
    spatial_reduced = spatial_reduce(
        jnp.concatenate([residual_block_output, lower_neighbor_row], axis=2),
        reduce_conv_weight,
        reduce_conv_bias,
    )
    alive_frame = (first_frame + jnp.arange(frames, dtype=jnp.int32))[None, :] < length[:, None]
    masked = jnp.where(alive_frame[:, :, None, None, None], spatial_reduced, 0.0).astype(
        jnp.bfloat16
    )
    return masked.reshape(batch, frames, band_rows // 2, columns // 2 * channels)


def general_local(
    features,
    lengths,
    stored_slot,
    owner_slot,
    gain_first,
    conv_first,
    bias_first,
    gain_second,
    conv_second,
    bias_second,
    reduce_conv_weight,
    reduce_conv_bias,
):
    local_count = features.shape[0]
    my_slots = lax.axis_index("clip") * local_count + jnp.arange(local_count, dtype=jnp.int32)
    numbers = jnp.arange(stored_slot.shape[0], dtype=jnp.int32)
    placed = (stored_slot[:, None] == numbers[None, :]).astype(jnp.int32)
    target = jnp.sum(placed * owner_slot[:, None], axis=0)
    hits = (stored_slot[None, :] == my_slots[:, None]).astype(jnp.int32)
    length = jnp.sum(hits * lengths[None, :], axis=1)
    local_out = encode(
        features,
        length,
        gain_first,
        conv_first,
        bias_first,
        gain_second,
        conv_second,
        bias_second,
        reduce_conv_weight,
        reduce_conv_bias,
    )
    shard_piece = lax.all_gather(local_out, "clip", axis=0, tiled=True)
    sources = jnp.arange(shard_piece.shape[0], dtype=jnp.int32)
    source_hits = (sources[:, None] == numbers[None, :]).astype(jnp.int32)
    goes_to = jnp.sum(source_hits * target[None, :], axis=1)
    weights = (goes_to[None, :] == my_slots[:, None]).astype(shard_piece.dtype)
    return jnp.einsum(
        "ki,iabc->kabc", weights, shard_piece, preferred_element_type=jnp.float32
    ).astype(shard_piece.dtype)


CHUNKS = 4


class Plan:
    def __init__(self, mesh, features, channels):
        self.blocks, self.bands, self.cores = (mesh.shape[a] for a in ("tm", "rows", "clip"))
        self.clips = features.shape[0] // self.cores
        self.frames = features.shape[1] // self.blocks
        self.band = features.shape[2] // self.bands
        self.all_frames, self.height = features.shape[1], features.shape[2]
        self.channels = channels
        self.width = features.shape[3] // channels
        self.parts = self.blocks
        self.own = self.width // self.parts
        self.window = self.own + LEFT + RIGHT
        self.pairs = self.window // 2
        self.devices = self.blocks * self.bands

    def fits(self):
        return (
            self.bands == self.clips
            and self.width % (2 * self.parts) == 0
            and 3 * (LANES - self.channels) == self.channels
            and self.band == 2
            and self.cores == 2
            and self.band * self.frames == 8
            and self.all_frames == 16
            and (self.window * self.channels) % LANES == 0
            and (self.width * self.channels) % LANES == 0
        )


def lanes_of(shape):
    return lax.broadcasted_iota(jnp.int32, shape, len(shape) - 1)


def spread_columns(plan, dense, column):
    start = column * plan.channels
    first, off = start // LANES * LANES, start % LANES
    value = dense[:, first : first + LANES]
    if off + plan.channels > LANES:
        following = dense[:, first + LANES : first + 2 * LANES]
        value = jnp.where(lanes_of(value.shape) >= off, value, following)
    if off:
        value = pltpu.roll(value, LANES - off, 1)
    return jnp.where(lanes_of(value.shape) < plan.channels, value, 0.0)


def merge_columns(plan, columns):
    rows = columns[0].shape[0]
    total = -(-len(columns) * plan.channels // LANES)
    merged = [None] * total
    for index, value in enumerate(columns):
        start = index * plan.channels
        first, off = start // LANES, start % LANES
        turned = pltpu.roll(value, off, 1) if off else value
        lane = lanes_of((rows, LANES))
        merged[first] = turned if off == 0 else jnp.where(lane >= off, turned, merged[first])
        if off + plan.channels > LANES:
            merged[first + 1] = turned
    return merged


def pack_kernel(plan, source_ref, out_ref, features_ref, wide_ref, copy_sems):
    channels, frames = plan.channels, plan.frames
    copies = [
        pltpu.make_async_copy(source_ref.at[clip], features_ref.at[clip], copy_sems.at[clip])
        for clip in range(plan.clips)
    ]
    for copy in copies:
        copy.start()
    lead = -(-LEFT * channels // LANES) * LANES
    inner = plan.width * channels
    ahead, count = lead // LANES, inner // LANES
    wide_ref[:, :ahead] = jnp.zeros((plan.clips, ahead, 8, LANES), jnp.float32)
    after = wide_ref.shape[1] - ahead - count
    wide_ref[:, ahead + count :] = jnp.zeros((plan.clips, after, 8, LANES), jnp.float32)
    for clip in range(plan.clips):
        copies[clip].wait()
        for frame in range(frames):
            rows = features_ref[clip, frame].astype(jnp.float32)
            for tile in range(count):
                wide_ref[clip, ahead + tile, pl.ds(frame, plan.band, stride=frames), :] = rows[
                    :, tile * LANES : (tile + 1) * LANES
                ]
        for q in range(plan.parts):
            start = lead + (q * plan.own - LEFT) * channels
            off = start % LANES
            for tile in range(plan.window * channels // LANES):
                first = start // LANES + tile
                value = wide_ref[clip, first]
                if off:
                    following = wide_ref[clip, first + 1]
                    value = jnp.where(lanes_of(value.shape) >= off, value, following)
                    value = pltpu.roll(value, LANES - off, 1)
                out_ref[q * plan.clips + clip, :, tile * LANES : (tile + 1) * LANES] = (
                    value.astype(jnp.bfloat16)
                )


def pack(plan, features):
    channels = plan.channels
    lead = -(-LEFT * channels // LANES) * LANES
    total = -(-(lead + (plan.width + RIGHT) * channels) // LANES)
    vmem = pl.BlockSpec(memory_space=pltpu.VMEM)
    return pl.pallas_call(
        functools.partial(pack_kernel, plan),
        out_shape=jax.ShapeDtypeStruct(
            (plan.devices, plan.band * plan.frames, plan.window * channels), jnp.bfloat16
        ),
        in_specs=[pl.BlockSpec(memory_space=pltpu.HBM)],
        out_specs=vmem,
        scratch_shapes=[
            pltpu.VMEM(features.shape, features.dtype),
            pltpu.VMEM((plan.clips, total, plan.band * plan.frames, LANES), jnp.float32),
            pltpu.SemaphoreType.DMA((plan.clips,)),
        ],
        compiler_params=pltpu.CompilerParams(vmem_limit_bytes=16 * 2**20),
    )(features)


def finish_kernel(plan, stored_ref, owner_ref, mine_ref, other_ref, out_ref):
    clips, channels = plan.clips, plan.channels
    core = lax.axis_index("clip")
    used = plan.own // 2 * channels
    lane = lanes_of((plan.frames, LANES))
    for place in range(clips):
        source = jnp.int32(0)
        for clip in range(stored_ref.shape[0]):
            here = owner_ref[clip] == core * clips + place
            source = source + jnp.where(here, stored_ref[clip], 0)
        local = source % clips
        is_mine = source // clips == core
        tiles = [None] * (plan.parts * used // LANES)
        for q in range(plan.parts):
            piece = jnp.where(
                is_mine, mine_ref[q * clips + local], other_ref[q * clips + local]
            ).astype(jnp.float32)
            first, off = q * used // LANES, q * used % LANES
            before = tiles[first] if off else None
            for index in range(piece.shape[1] // LANES):
                value = piece[:, index * LANES : (index + 1) * LANES]
                turned = pltpu.roll(value, off, 1) if off else value
                if first + index < len(tiles):
                    tiles[first + index] = jnp.where(lane >= off, turned, before) if off else turned
                before = turned
            if first + index + 1 < len(tiles):
                tiles[first + index + 1] = turned
        for index, value in enumerate(tiles):
            out_ref[place, :, index * LANES : (index + 1) * LANES] = value.astype(jnp.bfloat16)


def finish(plan, stored_slot, owner_slot, mine, other):
    vmem = pl.BlockSpec(memory_space=pltpu.VMEM)
    smem = pl.BlockSpec(memory_space=pltpu.SMEM)
    width = plan.parts * (plan.own // 2) * plan.channels
    return pl.pallas_call(
        functools.partial(finish_kernel, plan),
        out_shape=jax.ShapeDtypeStruct((plan.clips, plan.frames, width), jnp.bfloat16),
        in_specs=[smem, smem, vmem, vmem],
        out_specs=vmem,
        compiler_params=pltpu.CompilerParams(vmem_limit_bytes=16 * 2**20),
    )(stored_slot, owner_slot, mine, other)


def weight_rows():
    conv, reduction = 9 * 3 * LANES, 9 * LANES
    return conv, 2 * conv, 2 * conv + reduction


def spread_conv(plan, weight_ref, big_ref, base):
    channels = plan.channels
    spare = LANES - channels
    count = 9 * 3 * LANES
    big_ref[base : base + count] = jnp.zeros((count, 2 * LANES), big_ref.dtype)
    for tap in range(9):
        for side in range(2):
            for step in range(3):
                tile = side + step
                along = pl.ds(side * LANES, channels)
                if tile < 3:
                    first = base + (tap * 3 + tile) * LANES
                    big_ref[first : first + channels, along] = weight_ref[tap * 3 + step]
                    continue
                for tile in range(3):
                    first = base + (tap * 3 + tile) * LANES + channels
                    big_ref[first : first + spare, along] = weight_ref[
                        tap * 3 + step, tile * spare : (tile + 1) * spare
                    ]


def spread_reduction(plan, weight_ref, big_ref, base):
    big_ref[base:] = jnp.zeros_like(big_ref[base:])
    for tap in range(9):
        first = base + tap * LANES
        big_ref[first : first + plan.channels, 0 : plan.channels] = weight_ref[tap]


def encode_kernel(
    plan,
    lengths_ref,
    stored_ref,
    pieces_ref,
    conv_first_ref,
    conv_second_ref,
    conv_reduce_ref,
    gain_first_ref,
    bias_first_ref,
    gain_second_ref,
    bias_second_ref,
    bias_reduce_ref,
    out_ref,
    x_ref,
    act_first_ref,
    act_second_ref,
    wide_first_ref,
    wide_second_ref,
    conv_ref,
    block_ref,
    reduced_ref,
    vector_ref,
    weights_ref,
):
    frames, height, pairs, channels = plan.all_frames, plan.height, plan.pairs, plan.channels
    rows = height * frames
    part = lax.axis_index("tm")
    slot = lax.axis_index("clip") * plan.clips + lax.axis_index("rows")

    conv_rows, reduce_rows, end_rows = weight_rows()
    spread_conv(plan, conv_first_ref, weights_ref, 0)
    spread_conv(plan, conv_second_ref, weights_ref, conv_rows)
    spread_reduction(plan, conv_reduce_ref, weights_ref, reduce_rows)

    vector_ref[...] = jnp.zeros_like(vector_ref)
    for row, ref in enumerate(
        (gain_first_ref, bias_first_ref, gain_second_ref, bias_second_ref, bias_reduce_ref)
    ):
        vector_ref[row : row + 1, 0:channels] = ref[...]

    half = plan.frames
    sublane = lax.broadcasted_iota(jnp.int32, (8, LANES), 0)
    for band in range(plan.bands):
        dense = [
            pieces_ref[block * plan.bands + band].astype(jnp.float32)
            for block in range(plan.blocks)
        ]
        for column in range(plan.window):
            spread = [spread_columns(plan, piece, column) for piece in dense]
            turned = [pltpu.roll(value, half, 0) for value in spread]
            upper = [
                jnp.where(sublane < half, spread[2 * i], turned[2 * i + 1])
                for i in range(len(spread) // 2)
            ]
            lower = [
                jnp.where(sublane < half, turned[2 * i], spread[2 * i + 1])
                for i in range(len(spread) // 2)
            ]
            x_ref[column, 2 * band] = jnp.concatenate(upper, axis=0)
            x_ref[column, 2 * band + 1] = jnp.concatenate(lower, axis=0)

    def sum_matrix():
        shape = (2 * LANES, 2 * LANES)
        across = lax.broadcasted_iota(jnp.int32, shape, 0) // LANES
        along = lax.broadcasted_iota(jnp.int32, shape, 1) // LANES
        return jnp.where(across == along, 1.0, 0.0).astype(jnp.bfloat16)

    ones = sum_matrix()
    frame_of_row = lax.broadcasted_iota(jnp.int32, (rows, LANES), 0) % frames

    def in_image(pair):
        lane = lax.broadcasted_iota(jnp.int32, (1, 2 * LANES), 1)
        column = part * plan.own - LEFT + 2 * pair + lane // LANES
        return (column >= 0) & (column < plan.width)

    def activate(wide_ref, pair, values, gain):
        squares = (values * values).astype(jnp.bfloat16)
        sums = jnp.dot(squares, ones, preferred_element_type=jnp.float32)
        scale = jnp.where(in_image(pair), gain * (0.5 * channels**0.5), 0.0)
        scaled = values * lax.rsqrt(sums + channels * NORM_EPS) * scale
        wide_ref[pair + 1] = scaled + scaled * jnp.tanh(scaled)

    lane = lax.broadcasted_iota(jnp.int32, (rows, LANES), 1)

    def stack_window(wide_ref, act_ref, pair):
        before, after = wide_ref[pair, :, LANES:], wide_ref[pair + 2, :, :LANES]
        for tile, value in enumerate(
            (before, wide_ref[pair + 1, :, :LANES], wide_ref[pair + 1, :, LANES:])
        ):
            spill = pltpu.roll(after, channels - tile * (LANES - channels), 1)
            value = jnp.where(lane < channels, value, spill)
            for shift in range(3):
                moved = value
                if shift:
                    moved = jnp.where(frame_of_row >= shift, pltpu.roll(value, shift, 0), 0.0)
                act_ref[
                    2 - shift, pair, 1 : height + 1, :, tile * LANES : (tile + 1) * LANES
                ] = moved.astype(jnp.bfloat16).reshape(height, frames, LANES)

    def both(row):
        vector = vector_ref[row : row + 1, :]
        return jnp.concatenate([vector, vector], axis=1)

    first_weights = slice(0, conv_rows)
    second_weights = slice(conv_rows, reduce_rows)

    def convolve(act_ref, weights, first_pair, count):
        parts = [
            act_ref[
                tap // 3, first_pair : first_pair + count, tap % 3 : tap % 3 + height
            ].reshape(
                count * rows, 3 * LANES
            )
            for tap in range(9)
        ]
        stack = jnp.concatenate(parts, axis=1)
        return jnp.dot(stack, weights_ref[weights], preferred_element_type=jnp.float32)

    for act_ref in (act_first_ref, act_second_ref):
        act_ref[:, :, 0] = jnp.zeros_like(act_ref[:, :, 0])
        act_ref[:, :, height + 1] = jnp.zeros_like(act_ref[:, :, height + 1])
    wide_first_ref[0] = jnp.zeros_like(wide_first_ref[0])
    wide_second_ref[pairs] = jnp.zeros_like(wide_second_ref[pairs])
    block_ref[:, height] = jnp.zeros_like(block_ref[:, height])

    gain_first, gain_second = both(0), both(2)
    bias_first, bias_second = both(1), both(3)

    def first_window(acts, windows):
        for pair in acts:
            values = jnp.concatenate(
                [x_ref[2 * pair + side].reshape(rows, LANES) for side in range(2)], axis=1
            )
            activate(wide_first_ref, pair, values, gain_first)
        for pair in windows:
            stack_window(wide_first_ref, act_first_ref, pair)

    def second_window(acts, windows):
        for pair in acts:
            activate(wide_second_ref, pair, conv_ref[pair], gain_second)
        for pair in windows:
            stack_window(wide_second_ref, act_second_ref, pair)

    def first_conv(todo):
        result = convolve(act_first_ref, first_weights, todo[0], len(todo)) + bias_first
        for i, pair in enumerate(todo):
            conv_ref[pair] = result[i * rows : (i + 1) * rows]

    def second_conv(todo):
        result = convolve(act_second_ref, second_weights, todo[0], len(todo)) + bias_second
        for i, pair in enumerate(todo):
            for side in range(2):
                value = result[i * rows : (i + 1) * rows, side * LANES : (side + 1) * LANES]
                value = value.reshape(height, frames, LANES) + x_ref[2 * pair + side]
                column = part * plan.own - LEFT + 2 * pair + side
                value = jnp.where((column >= 0) & (column < plan.width), value, 0.0)
                block_ref[2 * pair + side, 0:height] = value.astype(jnp.bfloat16)

    outputs, half_rows = plan.own // 2, height // 2
    size = half_rows * frames

    def reduce_conv(todo):
        stacks = [
            jnp.concatenate(
                [
                    jnp.concatenate(
                        [
                            block_ref[LEFT + 2 * j + tap % 3, 2 * i + tap // 3]
                            for i in range(half_rows)
                        ],
                        axis=0,
                    )
                    for tap in range(9)
                ],
                axis=1,
            )
            for j in todo
        ]
        result = jnp.dot(
            jnp.concatenate(stacks, axis=0),
            weights_ref[reduce_rows:end_rows, 0:LANES],
            preferred_element_type=jnp.float32,
        )
        for i, j in enumerate(todo):
            reduced_ref[j] = result[i * size : (i + 1) * size] + vector_ref[4:5, :]

    last = pairs - 1
    cuts = [0] + [last * (i + 1) // CHUNKS for i in range(CHUNKS)]
    first_chunks = [range(a, b) for a, b in zip(cuts[:-1], cuts[1:])]
    second_cuts = [1] + [cut - 1 for cut in cuts[1:-1]] + [last]
    second_chunks = [range(a, b) for a, b in zip(second_cuts[:-1], second_cuts[1:])]
    done = 0
    reduced_until = 0
    for step in range(CHUNKS + 4):
        if 0 <= step - 1 < CHUNKS:
            first_conv(first_chunks[step - 1])
        if 0 <= step - 3 < CHUNKS and len(second_chunks[step - 3]):
            second_conv(second_chunks[step - 3])
        if 0 <= step - 4 < CHUNKS:
            until = min(second_chunks[step - 4].stop - 2, outputs)
            if until > reduced_until:
                reduce_conv(range(reduced_until, until))
                reduced_until = until
        if step < CHUNKS:
            until = first_chunks[step].stop + 1
            first_window(range(done, until), first_chunks[step])
            done = until
        if 0 <= step - 2 < CHUNKS:
            second_window(first_chunks[step - 2], second_chunks[step - 2])

    length = jnp.int32(0)
    for clip in range(lengths_ref.shape[0]):
        length = length + jnp.where(stored_ref[clip] == slot, lengths_ref[clip], 0)

    alive = lax.broadcasted_iota(jnp.int32, (half_rows * frames, LANES), 0) % frames < length
    merged = merge_columns(
        plan, [jnp.where(alive, reduced_ref[j], 0.0) for j in range(outputs)]
    )
    for tile, value in enumerate(merged):
        for i in range(half_rows):
            for block in range(plan.blocks):
                first = i * frames + block * plan.frames
                out_ref[block * plan.bands + i, :, tile * LANES : (tile + 1) * LANES] = value[
                    first : first + plan.frames
                ].astype(jnp.bfloat16)


def encode_window(
    plan, pieces, lengths, stored_slot, gain_first, conv_first, bias_first, gain_second,
    conv_second, bias_second, reduce_conv_weight, reduce_conv_bias,
):
    channels, pairs = plan.channels, plan.pairs
    rows = plan.height * plan.all_frames
    out_tiles = -(-plan.own // 2 * channels // LANES)
    vmem = pl.BlockSpec(memory_space=pltpu.VMEM)
    smem = pl.BlockSpec(memory_space=pltpu.SMEM)
    return pl.pallas_call(
        functools.partial(encode_kernel, plan),
        out_shape=jax.ShapeDtypeStruct(
            (plan.devices, plan.frames, out_tiles * LANES), jnp.bfloat16
        ),
        in_specs=[smem, smem] + [vmem] * 9,
        out_specs=vmem,
        scratch_shapes=[
            pltpu.VMEM((plan.window, plan.height, plan.all_frames, LANES), jnp.float32),
            pltpu.VMEM((3, pairs, plan.height + 2, plan.all_frames, 3 * LANES), jnp.bfloat16),
            pltpu.VMEM((3, pairs, plan.height + 2, plan.all_frames, 3 * LANES), jnp.bfloat16),
            pltpu.VMEM((pairs + 2, rows, 2 * LANES), jnp.float32),
            pltpu.VMEM((pairs + 2, rows, 2 * LANES), jnp.float32),
            pltpu.VMEM((pairs, rows, 2 * LANES), jnp.float32),
            pltpu.VMEM((plan.window, plan.height + 1, plan.all_frames, LANES), jnp.bfloat16),
            pltpu.VMEM((plan.own // 2, rows // 2, LANES), jnp.float32),
            pltpu.VMEM((8, LANES), jnp.float32),
            pltpu.VMEM((weight_rows()[2], 2 * LANES), jnp.bfloat16),
        ],
        compiler_params=pltpu.CompilerParams(vmem_limit_bytes=32 * 2**20),
    )(
        lengths,
        stored_slot,
        pieces,
        conv_first.reshape(27, channels, channels),
        conv_second.reshape(27, channels, channels),
        reduce_conv_weight.reshape(9, channels, channels),
        gain_first.reshape(1, channels),
        bias_first.reshape(1, channels),
        gain_second.reshape(1, channels),
        bias_second.reshape(1, channels),
        reduce_conv_bias.reshape(1, channels),
    )


def window_local(
    plan, features, lengths, stored_slot, owner_slot, gain_first, conv_first, bias_first,
    gain_second, conv_second, bias_second, reduce_conv_weight, reduce_conv_bias,
):
    clips = plan.clips
    pieces = pack(plan, features)
    pieces = lax.all_to_all(pieces, ("tm", "rows"), 0, 0, tiled=True)
    out = encode_window(
        plan, pieces, lengths, stored_slot, gain_first, conv_first, bias_first, gain_second,
        conv_second, bias_second, reduce_conv_weight, reduce_conv_bias,
    )
    out = lax.all_to_all(out, ("tm", "rows"), 0, 0, tiled=True)
    swap = [(core, plan.cores - 1 - core) for core in range(plan.cores)]
    other = lax.ppermute(out, "clip", swap)
    out = finish(plan, stored_slot, owner_slot, out, other)
    return out.reshape(clips, plan.frames, 1, out.shape[2])


def solution(mesh):
    out_specs = P("clip", "tm", "rows", None)
    in_specs = (out_specs,) + (P(),) * 11

    def run(features, *others):
        plan = Plan(mesh, features, others[3].shape[0])
        inner = functools.partial(window_local, plan) if plan.fits() else general_local
        return jax.shard_map(
            inner, mesh=mesh, in_specs=in_specs, out_specs=out_specs, check_vma=False
        )(features, *others)

    return run
```

```python
import functools

import jax
import jax.numpy as jnp
from jax import lax
from jax.experimental import pallas as pl
from jax.experimental.pallas import tpu as pltpu
from jax.sharding import PartitionSpec as P

NORM_EPS = 1e-06
LANES = 128
LEFT, RIGHT = 2, 4


def from_behind(value, axis, steps):
    count = lax.axis_size(axis)
    first, last = (max(0, -steps), min(count, count - steps))
    return lax.ppermute(value, axis, [(source, source + steps) for source in range(first, last)])


def padded_2(x, sides, width):
    for axis, dim in sides:
        count, length = (lax.axis_size(axis), x.shape[dim])
        up = [(i, (i + 1) % count) for i in range(count - 1)]
        down = [(j, i) for i, j in up]
        last = lax.slice_in_dim(x, length - width, length, axis=dim)
        first = lax.slice_in_dim(x, 0, width, axis=dim)
        before = lax.ppermute(last, axis, up)
        after = lax.ppermute(first, axis, down)
        x = jnp.concatenate([before, x, after], axis=dim)
    return x


def norm_silu(values, gain_vec):
    scaled = (
        values * lax.rsqrt(jnp.mean(values * values, axis=-1, keepdims=True) + NORM_EPS) * gain_vec
    )
    return jax.nn.silu(scaled)


def conv_valid(grown_block, kernel_weight, bias_vector):
    batch = grown_block.shape[0]
    frames = grown_block.shape[1] - 2
    band_rows = grown_block.shape[2] - 2
    columns = grown_block.shape[3]
    channels = grown_block.shape[4]
    outputs = kernel_weight.shape[4]
    padded = jnp.pad(grown_block, ((0, 0), (0, 0), (0, 0), (1, 1), (0, 0)))
    running_sum = jnp.zeros((batch * frames * band_rows * columns, outputs), jnp.float32)
    for step_t in range(3):
        for step_h in range(3):
            window = padded[:, step_t : step_t + frames, step_h : step_h + band_rows]
            tap_stack = jnp.concatenate(
                [window[:, :, :, step_w : step_w + columns] for step_w in range(3)], axis=-1
            )
            running_sum = running_sum + jnp.dot(
                tap_stack.reshape(-1, 3 * channels),
                kernel_weight[step_t, step_h].reshape(3 * channels, outputs),
                preferred_element_type=jnp.float32,
            )
    return (running_sum + bias_vector).reshape(batch, frames, band_rows, columns, outputs)


def spatial_reduce(padded_frames, kernel_weight, bias_vector):
    batch = padded_frames.shape[0]
    frames = padded_frames.shape[1]
    half_rows = (padded_frames.shape[2] - 1) // 2
    columns = padded_frames.shape[3]
    channels = padded_frames.shape[4]
    outputs = kernel_weight.shape[3]
    padded = jnp.pad(padded_frames, ((0, 0), (0, 0), (0, 0), (0, 1), (0, 0)))
    running_sum = jnp.zeros((batch * frames * half_rows * (columns // 2), outputs), jnp.float32)
    for step_h in range(3):
        row_band = padded[:, :, step_h : step_h + 2 * half_rows - 1 : 2]
        tap_stack = jnp.concatenate(
            [row_band[:, :, :, step_w : step_w + columns - 1 : 2] for step_w in range(3)], axis=-1
        )
        running_sum = running_sum + jnp.dot(
            tap_stack.reshape(-1, 3 * channels),
            kernel_weight[step_h].reshape(3 * channels, outputs),
            preferred_element_type=jnp.float32,
        )
    return (running_sum + bias_vector).reshape(batch, frames, half_rows, columns // 2, outputs)


def encode(
    clip_block,
    length,
    gain_first,
    conv_first,
    bias_first,
    gain_second,
    conv_second,
    bias_second,
    reduce_conv_weight,
    reduce_conv_bias,
):
    batch = clip_block.shape[0]
    frames = clip_block.shape[1]
    band_rows = clip_block.shape[2]
    channels = gain_first.shape[0]
    columns = clip_block.shape[3] // channels
    feature_map = clip_block.reshape(batch, frames, band_rows, columns, channels)
    first_frame = lax.axis_index("tm") * frames
    first_act = norm_silu(feature_map.astype(jnp.float32), gain_first).astype(jnp.bfloat16)
    earlier = from_behind(first_act[:, frames - 2 :], "tm", 1)
    grown_block = padded_2(jnp.concatenate([earlier, first_act], axis=1), (("rows", 2),), 1)
    first_conv = conv_valid(grown_block, conv_first, bias_first)
    second_act = norm_silu(first_conv, gain_second).astype(jnp.bfloat16)
    earlier_two = from_behind(second_act[:, frames - 2 :], "tm", 1)
    grown_two = padded_2(jnp.concatenate([earlier_two, second_act], axis=1), (("rows", 2),), 1)
    branch = conv_valid(grown_two, conv_second, bias_second)
    residual_block_output = (feature_map.astype(jnp.float32) + branch).astype(jnp.bfloat16)
    lower_neighbor_row = from_behind(residual_block_output[:, :, :1], "rows", -1)
    spatial_reduced = spatial_reduce(
        jnp.concatenate([residual_block_output, lower_neighbor_row], axis=2),
        reduce_conv_weight,
        reduce_conv_bias,
    )
    alive_frame = (first_frame + jnp.arange(frames, dtype=jnp.int32))[None, :] < length[:, None]
    masked = jnp.where(alive_frame[:, :, None, None, None], spatial_reduced, 0.0).astype(
        jnp.bfloat16
    )
    return masked.reshape(batch, frames, band_rows // 2, columns // 2 * channels)


def general_local(
    features,
    lengths,
    stored_slot,
    owner_slot,
    gain_first,
    conv_first,
    bias_first,
    gain_second,
    conv_second,
    bias_second,
    reduce_conv_weight,
    reduce_conv_bias,
):
    local_count = features.shape[0]
    my_slots = lax.axis_index("clip") * local_count + jnp.arange(local_count, dtype=jnp.int32)
    numbers = jnp.arange(stored_slot.shape[0], dtype=jnp.int32)
    placed = (stored_slot[:, None] == numbers[None, :]).astype(jnp.int32)
    target = jnp.sum(placed * owner_slot[:, None], axis=0)
    hits = (stored_slot[None, :] == my_slots[:, None]).astype(jnp.int32)
    length = jnp.sum(hits * lengths[None, :], axis=1)
    local_out = encode(
        features,
        length,
        gain_first,
        conv_first,
        bias_first,
        gain_second,
        conv_second,
        bias_second,
        reduce_conv_weight,
        reduce_conv_bias,
    )
    shard_piece = lax.all_gather(local_out, "clip", axis=0, tiled=True)
    sources = jnp.arange(shard_piece.shape[0], dtype=jnp.int32)
    source_hits = (sources[:, None] == numbers[None, :]).astype(jnp.int32)
    goes_to = jnp.sum(source_hits * target[None, :], axis=1)
    weights = (goes_to[None, :] == my_slots[:, None]).astype(shard_piece.dtype)
    return jnp.einsum(
        "ki,iabc->kabc", weights, shard_piece, preferred_element_type=jnp.float32
    ).astype(shard_piece.dtype)


CUTS = (4, 8, 12, 15)
CHUNKS = len(CUTS)


class Plan:
    def __init__(self, mesh, features, channels):
        self.blocks, self.bands, self.cores = (mesh.shape[a] for a in ("tm", "rows", "clip"))
        self.clips = features.shape[0] // self.cores
        self.frames = features.shape[1] // self.blocks
        self.band = features.shape[2] // self.bands
        self.all_frames, self.height = features.shape[1], features.shape[2]
        self.channels = channels
        self.width = features.shape[3] // channels
        self.parts = self.blocks
        self.own = self.width // self.parts
        self.window = self.own + LEFT + RIGHT
        self.pairs = self.window // 2
        self.devices = self.blocks * self.bands

    def fits(self):
        return (
            self.bands == self.clips
            and self.width % (2 * self.parts) == 0
            and 3 * (LANES - self.channels) == self.channels
            and self.band == 2
            and self.cores == 2
            and self.band * self.frames == 8
            and self.all_frames == 16
            and (self.window * self.channels) % LANES == 0
            and (self.width * self.channels) % LANES == 0
        )


def lanes_of(shape):
    return lax.broadcasted_iota(jnp.int32, shape, len(shape) - 1)


def spread_columns(plan, dense, column):
    start = column * plan.channels
    first, off = start // LANES * LANES, start % LANES
    value = dense[:, first : first + LANES]
    if off + plan.channels > LANES:
        following = dense[:, first + LANES : first + 2 * LANES]
        value = jnp.where(lanes_of(value.shape) >= off, value, following)
    if off:
        value = pltpu.roll(value, LANES - off, 1)
    return jnp.where(lanes_of(value.shape) < plan.channels, value, 0.0)


def merge_columns(plan, columns):
    rows = columns[0].shape[0]
    total = -(-len(columns) * plan.channels // LANES)
    merged = [None] * total
    for index, value in enumerate(columns):
        start = index * plan.channels
        first, off = start // LANES, start % LANES
        turned = pltpu.roll(value, off, 1) if off else value
        lane = lanes_of((rows, LANES))
        merged[first] = turned if off == 0 else jnp.where(lane >= off, turned, merged[first])
        if off + plan.channels > LANES:
            merged[first + 1] = turned
    return merged


def slot_source(plan, stored_ref, owner_ref, place):
    wanted = lax.axis_index("clip") * plan.clips + place
    source = jnp.int32(0)
    for clip in range(stored_ref.shape[0]):
        source = source + jnp.where(owner_ref[clip] == wanted, stored_ref[clip], 0)
    return source


def vectors_kernel(
    plan, lengths_ref, stored_ref, owner_ref, gain_first_ref, bias_first_ref, gain_second_ref,
    bias_second_ref, bias_reduce_ref, vector_ref,
):
    vector_ref[...] = jnp.zeros_like(vector_ref)
    for row, ref in enumerate(
        (gain_first_ref, bias_first_ref, gain_second_ref, bias_second_ref, bias_reduce_ref)
    ):
        vector_ref[row : row + 1, 0 : plan.channels] = ref[...]
    wanted = lax.axis_index("clip") * plan.clips + lax.axis_index("rows")
    length = jnp.int32(0)
    for clip in range(lengths_ref.shape[0]):
        length = length + jnp.where(owner_ref[clip] == wanted, lengths_ref[clip], 0)
    vector_ref[5:6, :] = jnp.full((1, LANES), length, jnp.int32).astype(jnp.float32)


def gather_vectors(plan, lengths, stored_slot, owner_slot, vectors):
    vmem = pl.BlockSpec(memory_space=pltpu.VMEM)
    smem = pl.BlockSpec(memory_space=pltpu.SMEM)
    return pl.pallas_call(
        functools.partial(vectors_kernel, plan),
        out_shape=jax.ShapeDtypeStruct((8, LANES), jnp.float32),
        in_specs=[smem] * 3 + [vmem] * 5,
        out_specs=vmem,
        compiler_params=pltpu.CompilerParams(vmem_limit_bytes=4 * 2**20),
    )(
        lengths,
        stored_slot,
        owner_slot,
        *(vector.reshape(1, plan.channels) for vector in vectors),
    )


def pack_kernel(plan, stored_ref, owner_ref, vector_ref, mine_ref, other_ref, out_ref, wide_ref):
    channels, frames = plan.channels, plan.frames
    lead = -(-LEFT * channels // LANES) * LANES
    inner = plan.width * channels
    ahead, count = lead // LANES, inner // LANES
    wide_ref[:, :ahead] = jnp.zeros((plan.clips, ahead, 8, LANES), jnp.float32)
    after = wide_ref.shape[1] - ahead - count
    wide_ref[:, ahead + count :] = jnp.zeros((plan.clips, after, 8, LANES), jnp.float32)
    for clip in range(plan.clips):
        source = slot_source(plan, stored_ref, owner_ref, clip)
        local = source % plan.clips
        is_mine = source // plan.clips == lax.axis_index("clip")

        def spread_frames(features_ref):
            for frame in range(frames):
                rows = features_ref[local, frame].astype(jnp.float32)
                for tile in range(count):
                    wide_ref[clip, ahead + tile, pl.ds(frame, plan.band, stride=frames), :] = rows[
                        :, tile * LANES : (tile + 1) * LANES
                    ]

        @pl.when(is_mine)
        def _():
            spread_frames(mine_ref)

        @pl.when(jnp.logical_not(is_mine))
        def _():
            spread_frames(other_ref)

        for q in range(plan.parts):
            start = lead + (q * plan.own - LEFT) * channels
            off = start % LANES
            for tile in range(plan.window * channels // LANES):
                first = start // LANES + tile
                value = wide_ref[clip, first]
                if off:
                    following = wide_ref[clip, first + 1]
                    value = jnp.where(lanes_of(value.shape) >= off, value, following)
                    value = pltpu.roll(value, LANES - off, 1)
                out_ref[clip * plan.parts + q, :, tile * LANES : (tile + 1) * LANES] = (
                    value.astype(jnp.bfloat16)
                )


def pack(plan, stored_slot, owner_slot, vectors, mine, other):
    channels = plan.channels
    lead = -(-LEFT * channels // LANES) * LANES
    total = -(-(lead + (plan.width + RIGHT) * channels) // LANES)
    vmem = pl.BlockSpec(memory_space=pltpu.VMEM)
    smem = pl.BlockSpec(memory_space=pltpu.SMEM)
    piece_rows = plan.band * plan.frames
    return pl.pallas_call(
        functools.partial(pack_kernel, plan),
        out_shape=jax.ShapeDtypeStruct(
            (plan.devices, piece_rows, plan.window * channels), jnp.bfloat16
        ),
        in_specs=[smem, smem, pl.BlockSpec(memory_space=pl.ANY), vmem, vmem],
        out_specs=vmem,
        scratch_shapes=[pltpu.VMEM((plan.clips, total, piece_rows, LANES), jnp.float32)],
        compiler_params=pltpu.CompilerParams(vmem_limit_bytes=16 * 2**20),
    )(stored_slot, owner_slot, vectors, mine, other)


def finish_kernel(plan, pieces_ref, out_ref):
    clips, channels = plan.clips, plan.channels
    used = plan.own // 2 * channels
    lane = lanes_of((plan.frames, LANES))
    for place in range(clips):
        tiles = [None] * (plan.parts * used // LANES)
        for q in range(plan.parts):
            piece = pieces_ref[place * plan.parts + q].astype(jnp.float32)
            first, off = q * used // LANES, q * used % LANES
            before = tiles[first] if off else None
            for index in range(piece.shape[1] // LANES):
                value = piece[:, index * LANES : (index + 1) * LANES]
                turned = pltpu.roll(value, off, 1) if off else value
                if first + index < len(tiles):
                    tiles[first + index] = jnp.where(lane >= off, turned, before) if off else turned
                before = turned
            if first + index + 1 < len(tiles):
                tiles[first + index + 1] = turned
        for index, value in enumerate(tiles):
            out_ref[place, :, index * LANES : (index + 1) * LANES] = value.astype(jnp.bfloat16)


def finish(plan, pieces):
    vmem = pl.BlockSpec(memory_space=pltpu.VMEM)
    width = plan.parts * (plan.own // 2) * plan.channels
    return pl.pallas_call(
        functools.partial(finish_kernel, plan),
        out_shape=jax.ShapeDtypeStruct((plan.clips, plan.frames, width), jnp.bfloat16),
        in_specs=[vmem],
        out_specs=vmem,
        compiler_params=pltpu.CompilerParams(vmem_limit_bytes=16 * 2**20),
    )(pieces)


def weight_rows():
    conv, reduction = 9 * 3 * LANES, 9 * LANES
    return conv, 2 * conv, 2 * conv + reduction


def spread_conv(plan, weight_ref, big_ref, base):
    channels = plan.channels
    spare = LANES - channels
    count = 9 * 3 * LANES
    big_ref[base : base + count] = jnp.zeros((count, 2 * LANES), big_ref.dtype)
    for tap in range(9):
        for side in range(2):
            for step in range(3):
                tile = side + step
                along = pl.ds(side * LANES, channels)
                if tile < 3:
                    first = base + (tap * 3 + tile) * LANES
                    big_ref[first : first + channels, along] = weight_ref[tap * 3 + step]
                    continue
                for tile in range(3):
                    first = base + (tap * 3 + tile) * LANES + channels
                    big_ref[first : first + spare, along] = weight_ref[
                        tap * 3 + step, tile * spare : (tile + 1) * spare
                    ]


def spread_reduction(plan, weight_ref, big_ref, base):
    big_ref[base:] = jnp.zeros_like(big_ref[base:])
    for tap in range(9):
        first = base + tap * LANES
        big_ref[first : first + plan.channels, 0 : plan.channels] = weight_ref[tap]


def encode_kernel(
    plan,
    pieces_ref,
    vector_ref,
    conv_first_ref,
    conv_second_ref,
    conv_reduce_ref,
    out_ref,
    x_ref,
    act_first_ref,
    act_second_ref,
    wide_first_ref,
    wide_second_ref,
    conv_ref,
    block_ref,
    reduced_ref,
    weights_ref,
):
    frames, height, pairs, channels = plan.all_frames, plan.height, plan.pairs, plan.channels
    rows = height * frames
    part = lax.axis_index("tm")

    conv_rows, reduce_rows, end_rows = weight_rows()
    spread_conv(plan, conv_first_ref, weights_ref, 0)
    spread_conv(plan, conv_second_ref, weights_ref, conv_rows)
    spread_reduction(plan, conv_reduce_ref, weights_ref, reduce_rows)

    half = plan.frames
    sublane = lax.broadcasted_iota(jnp.int32, (8, LANES), 0)
    for band in range(plan.bands):
        dense = [
            pieces_ref[band * plan.blocks + block].astype(jnp.float32)
            for block in range(plan.blocks)
        ]
        for column in range(plan.window):
            spread = [spread_columns(plan, piece, column) for piece in dense]
            turned = [pltpu.roll(value, half, 0) for value in spread]
            upper = [
                jnp.where(sublane < half, spread[2 * i], turned[2 * i + 1])
                for i in range(len(spread) // 2)
            ]
            lower = [
                jnp.where(sublane < half, turned[2 * i], spread[2 * i + 1])
                for i in range(len(spread) // 2)
            ]
            x_ref[column, 2 * band] = jnp.concatenate(upper, axis=0)
            x_ref[column, 2 * band + 1] = jnp.concatenate(lower, axis=0)

    def sum_matrix():
        shape = (2 * LANES, 2 * LANES)
        across = lax.broadcasted_iota(jnp.int32, shape, 0) // LANES
        along = lax.broadcasted_iota(jnp.int32, shape, 1) // LANES
        return jnp.where(across == along, 1.0, 0.0).astype(jnp.bfloat16)

    ones = sum_matrix()
    frame_of_row = lax.broadcasted_iota(jnp.int32, (rows, LANES), 0) % frames

    def in_image(pair):
        lane = lax.broadcasted_iota(jnp.int32, (1, 2 * LANES), 1)
        column = part * plan.own - LEFT + 2 * pair + lane // LANES
        return (column >= 0) & (column < plan.width)

    def activate(wide_ref, pair, values, gain):
        squares = (values * values).astype(jnp.bfloat16)
        sums = jnp.dot(squares, ones, preferred_element_type=jnp.float32)
        scale = jnp.where(in_image(pair), gain * (0.5 * channels**0.5), 0.0)
        scaled = values * lax.rsqrt(sums + channels * NORM_EPS) * scale
        wide_ref[pair + 1] = scaled + scaled * jnp.tanh(scaled)

    lane = lax.broadcasted_iota(jnp.int32, (rows, LANES), 1)

    def stack_window(wide_ref, act_ref, pair):
        before, after = wide_ref[pair, :, LANES:], wide_ref[pair + 2, :, :LANES]
        for tile, value in enumerate(
            (before, wide_ref[pair + 1, :, :LANES], wide_ref[pair + 1, :, LANES:])
        ):
            spill = pltpu.roll(after, channels - tile * (LANES - channels), 1)
            value = jnp.where(lane < channels, value, spill)
            for shift in range(3):
                moved = value
                if shift:
                    moved = jnp.where(frame_of_row >= shift, pltpu.roll(value, shift, 0), 0.0)
                act_ref[
                    2 - shift, pair, 1 : height + 1, :, tile * LANES : (tile + 1) * LANES
                ] = moved.astype(jnp.bfloat16).reshape(height, frames, LANES)

    def both(row):
        vector = vector_ref[row : row + 1, :]
        return jnp.concatenate([vector, vector], axis=1)

    first_weights = slice(0, conv_rows)
    second_weights = slice(conv_rows, reduce_rows)

    def convolve(act_ref, weights, first_pair, count):
        parts = [
            act_ref[
                tap // 3, first_pair : first_pair + count, tap % 3 : tap % 3 + height
            ].reshape(
                count * rows, 3 * LANES
            )
            for tap in range(9)
        ]
        stack = jnp.concatenate(parts, axis=1)
        return jnp.dot(stack, weights_ref[weights], preferred_element_type=jnp.float32)

    for act_ref in (act_first_ref, act_second_ref):
        act_ref[:, :, 0] = jnp.zeros_like(act_ref[:, :, 0])
        act_ref[:, :, height + 1] = jnp.zeros_like(act_ref[:, :, height + 1])
    wide_first_ref[0] = jnp.zeros_like(wide_first_ref[0])
    wide_second_ref[pairs] = jnp.zeros_like(wide_second_ref[pairs])
    block_ref[:, height] = jnp.zeros_like(block_ref[:, height])

    gain_first, gain_second = both(0), both(2)
    bias_first, bias_second = both(1), both(3)

    def first_window(acts, windows):
        for pair in acts:
            values = jnp.concatenate(
                [x_ref[2 * pair + side].reshape(rows, LANES) for side in range(2)], axis=1
            )
            activate(wide_first_ref, pair, values, gain_first)
        for pair in windows:
            stack_window(wide_first_ref, act_first_ref, pair)

    def second_window(acts, windows):
        for pair in acts:
            activate(wide_second_ref, pair, conv_ref[pair], gain_second)
        for pair in windows:
            stack_window(wide_second_ref, act_second_ref, pair)

    def first_conv(todo):
        result = convolve(act_first_ref, first_weights, todo[0], len(todo)) + bias_first
        for i, pair in enumerate(todo):
            conv_ref[pair] = result[i * rows : (i + 1) * rows]

    def second_conv(todo):
        result = convolve(act_second_ref, second_weights, todo[0], len(todo)) + bias_second
        for i, pair in enumerate(todo):
            for side in range(2):
                value = result[i * rows : (i + 1) * rows, side * LANES : (side + 1) * LANES]
                value = value.reshape(height, frames, LANES) + x_ref[2 * pair + side]
                column = part * plan.own - LEFT + 2 * pair + side
                value = jnp.where((column >= 0) & (column < plan.width), value, 0.0)
                block_ref[2 * pair + side, 0:height] = value.astype(jnp.bfloat16)

    outputs, half_rows = plan.own // 2, height // 2
    size = half_rows * frames

    def reduce_conv(todo):
        stacks = [
            jnp.concatenate(
                [
                    jnp.concatenate(
                        [
                            block_ref[LEFT + 2 * j + tap % 3, 2 * i + tap // 3]
                            for i in range(half_rows)
                        ],
                        axis=0,
                    )
                    for tap in range(9)
                ],
                axis=1,
            )
            for j in todo
        ]
        result = jnp.dot(
            jnp.concatenate(stacks, axis=0),
            weights_ref[reduce_rows:end_rows, 0:LANES],
            preferred_element_type=jnp.float32,
        )
        for i, j in enumerate(todo):
            reduced_ref[j] = result[i * size : (i + 1) * size] + vector_ref[4:5, :]

    last = pairs - 1
    cuts = [0] + [last * end // CUTS[-1] for end in CUTS]
    first_chunks = [range(a, b) for a, b in zip(cuts[:-1], cuts[1:])]
    second_cuts = [1] + [cut - 1 for cut in cuts[1:-1]] + [last]
    second_chunks = [range(a, b) for a, b in zip(second_cuts[:-1], second_cuts[1:])]
    done = 0
    reduced_until = 0
    for step in range(CHUNKS + 4):
        if 0 <= step - 1 < CHUNKS:
            first_conv(first_chunks[step - 1])
        if 0 <= step - 3 < CHUNKS and len(second_chunks[step - 3]):
            second_conv(second_chunks[step - 3])
        if 0 <= step - 4 < CHUNKS:
            until = min(second_chunks[step - 4].stop - 2, outputs)
            if until > reduced_until:
                reduce_conv(range(reduced_until, until))
                reduced_until = until
        if step < CHUNKS:
            until = first_chunks[step].stop + 1
            first_window(range(done, until), first_chunks[step])
            done = until
        if 0 <= step - 2 < CHUNKS:
            second_window(first_chunks[step - 2], second_chunks[step - 2])

    alive = lax.broadcasted_iota(jnp.int32, (size, LANES), 0) % frames
    alive = alive.astype(jnp.float32) < vector_ref[5:6, :]
    merged = merge_columns(
        plan, [jnp.where(alive, reduced_ref[j], 0.0) for j in range(outputs)]
    )
    for tile, value in enumerate(merged):
        for i in range(half_rows):
            for block in range(plan.blocks):
                first = i * frames + block * plan.frames
                out_ref[i * plan.blocks + block, :, tile * LANES : (tile + 1) * LANES] = value[
                    first : first + plan.frames
                ].astype(jnp.bfloat16)


def encode_window(plan, pieces, vectors, conv_first, conv_second, reduce_conv_weight):
    channels, pairs = plan.channels, plan.pairs
    rows = plan.height * plan.all_frames
    out_tiles = -(-plan.own // 2 * channels // LANES)
    vmem = pl.BlockSpec(memory_space=pltpu.VMEM)
    acts = pltpu.VMEM((3, pairs, plan.height + 2, plan.all_frames, 3 * LANES), jnp.bfloat16)
    wide = pltpu.VMEM((pairs + 2, rows, 2 * LANES), jnp.float32)
    return pl.pallas_call(
        functools.partial(encode_kernel, plan),
        out_shape=jax.ShapeDtypeStruct(
            (plan.devices, plan.frames, out_tiles * LANES), jnp.bfloat16
        ),
        in_specs=[vmem] * 5,
        out_specs=vmem,
        scratch_shapes=[
            pltpu.VMEM((plan.window, plan.height, plan.all_frames, LANES), jnp.float32),
            acts,
            acts,
            wide,
            wide,
            pltpu.VMEM((pairs, rows, 2 * LANES), jnp.float32),
            pltpu.VMEM((plan.window, plan.height + 1, plan.all_frames, LANES), jnp.bfloat16),
            pltpu.VMEM((plan.own // 2, rows // 2, LANES), jnp.float32),
            pltpu.VMEM((weight_rows()[2], 2 * LANES), jnp.bfloat16),
        ],
        compiler_params=pltpu.CompilerParams(vmem_limit_bytes=32 * 2**20),
    )(
        pieces,
        vectors,
        conv_first.reshape(27, channels, channels),
        conv_second.reshape(27, channels, channels),
        reduce_conv_weight.reshape(9, channels, channels),
    )


def window_local(
    plan, features, lengths, stored_slot, owner_slot, gain_first, conv_first, bias_first,
    gain_second, conv_second, bias_second, reduce_conv_weight, reduce_conv_bias,
):
    swap = [(core, plan.cores - 1 - core) for core in range(plan.cores)]
    other = lax.ppermute(features, "clip", swap)
    vectors = (gain_first, bias_first, gain_second, bias_second, reduce_conv_bias)
    vectors = gather_vectors(plan, lengths, stored_slot, owner_slot, vectors)
    pieces = pack(plan, stored_slot, owner_slot, vectors, features, other)
    pieces = lax.all_to_all(pieces, ("rows", "tm"), 0, 0, tiled=True)
    out = encode_window(plan, pieces, vectors, conv_first, conv_second, reduce_conv_weight)
    out = lax.all_to_all(out, ("rows", "tm"), 0, 0, tiled=True)
    out = finish(plan, out)
    return out.reshape(plan.clips, plan.frames, 1, out.shape[2])


def solution(mesh):
    out_specs = P("clip", "tm", "rows", None)
    in_specs = (out_specs,) + (P(),) * 11

    def run(features, *others):
        plan = Plan(mesh, features, others[3].shape[0])
        inner = functools.partial(window_local, plan) if plan.fits() else general_local
        return jax.shard_map(
            inner, mesh=mesh, in_specs=in_specs, out_specs=out_specs, check_vma=False
        )(features, *others)

    return run
```

```python
import functools

import jax
import jax.numpy as jnp
from jax import lax
from jax.experimental import pallas as pl
from jax.experimental.pallas import tpu as pltpu
from jax.sharding import PartitionSpec as P

NORM_EPS = 1e-06
LANES = 128
LEFT, RIGHT = 2, 4


def from_behind(value, axis, steps):
    count = lax.axis_size(axis)
    first, last = (max(0, -steps), min(count, count - steps))
    return lax.ppermute(value, axis, [(source, source + steps) for source in range(first, last)])


def padded_2(x, sides, width):
    for axis, dim in sides:
        count, length = (lax.axis_size(axis), x.shape[dim])
        up = [(i, (i + 1) % count) for i in range(count - 1)]
        down = [(j, i) for i, j in up]
        last = lax.slice_in_dim(x, length - width, length, axis=dim)
        first = lax.slice_in_dim(x, 0, width, axis=dim)
        before = lax.ppermute(last, axis, up)
        after = lax.ppermute(first, axis, down)
        x = jnp.concatenate([before, x, after], axis=dim)
    return x


def norm_silu(values, gain_vec):
    scaled = (
        values * lax.rsqrt(jnp.mean(values * values, axis=-1, keepdims=True) + NORM_EPS) * gain_vec
    )
    return jax.nn.silu(scaled)


def conv_valid(grown_block, kernel_weight, bias_vector):
    batch = grown_block.shape[0]
    frames = grown_block.shape[1] - 2
    band_rows = grown_block.shape[2] - 2
    columns = grown_block.shape[3]
    channels = grown_block.shape[4]
    outputs = kernel_weight.shape[4]
    padded = jnp.pad(grown_block, ((0, 0), (0, 0), (0, 0), (1, 1), (0, 0)))
    running_sum = jnp.zeros((batch * frames * band_rows * columns, outputs), jnp.float32)
    for step_t in range(3):
        for step_h in range(3):
            window = padded[:, step_t : step_t + frames, step_h : step_h + band_rows]
            tap_stack = jnp.concatenate(
                [window[:, :, :, step_w : step_w + columns] for step_w in range(3)], axis=-1
            )
            running_sum = running_sum + jnp.dot(
                tap_stack.reshape(-1, 3 * channels),
                kernel_weight[step_t, step_h].reshape(3 * channels, outputs),
                preferred_element_type=jnp.float32,
            )
    return (running_sum + bias_vector).reshape(batch, frames, band_rows, columns, outputs)


def spatial_reduce(padded_frames, kernel_weight, bias_vector):
    batch = padded_frames.shape[0]
    frames = padded_frames.shape[1]
    half_rows = (padded_frames.shape[2] - 1) // 2
    columns = padded_frames.shape[3]
    channels = padded_frames.shape[4]
    outputs = kernel_weight.shape[3]
    padded = jnp.pad(padded_frames, ((0, 0), (0, 0), (0, 0), (0, 1), (0, 0)))
    running_sum = jnp.zeros((batch * frames * half_rows * (columns // 2), outputs), jnp.float32)
    for step_h in range(3):
        row_band = padded[:, :, step_h : step_h + 2 * half_rows - 1 : 2]
        tap_stack = jnp.concatenate(
            [row_band[:, :, :, step_w : step_w + columns - 1 : 2] for step_w in range(3)], axis=-1
        )
        running_sum = running_sum + jnp.dot(
            tap_stack.reshape(-1, 3 * channels),
            kernel_weight[step_h].reshape(3 * channels, outputs),
            preferred_element_type=jnp.float32,
        )
    return (running_sum + bias_vector).reshape(batch, frames, half_rows, columns // 2, outputs)


def encode(
    clip_block,
    length,
    gain_first,
    conv_first,
    bias_first,
    gain_second,
    conv_second,
    bias_second,
    reduce_conv_weight,
    reduce_conv_bias,
):
    batch = clip_block.shape[0]
    frames = clip_block.shape[1]
    band_rows = clip_block.shape[2]
    channels = gain_first.shape[0]
    columns = clip_block.shape[3] // channels
    feature_map = clip_block.reshape(batch, frames, band_rows, columns, channels)
    first_frame = lax.axis_index("tm") * frames
    first_act = norm_silu(feature_map.astype(jnp.float32), gain_first).astype(jnp.bfloat16)
    earlier = from_behind(first_act[:, frames - 2 :], "tm", 1)
    grown_block = padded_2(jnp.concatenate([earlier, first_act], axis=1), (("rows", 2),), 1)
    first_conv = conv_valid(grown_block, conv_first, bias_first)
    second_act = norm_silu(first_conv, gain_second).astype(jnp.bfloat16)
    earlier_two = from_behind(second_act[:, frames - 2 :], "tm", 1)
    grown_two = padded_2(jnp.concatenate([earlier_two, second_act], axis=1), (("rows", 2),), 1)
    branch = conv_valid(grown_two, conv_second, bias_second)
    residual_block_output = (feature_map.astype(jnp.float32) + branch).astype(jnp.bfloat16)
    lower_neighbor_row = from_behind(residual_block_output[:, :, :1], "rows", -1)
    spatial_reduced = spatial_reduce(
        jnp.concatenate([residual_block_output, lower_neighbor_row], axis=2),
        reduce_conv_weight,
        reduce_conv_bias,
    )
    alive_frame = (first_frame + jnp.arange(frames, dtype=jnp.int32))[None, :] < length[:, None]
    masked = jnp.where(alive_frame[:, :, None, None, None], spatial_reduced, 0.0).astype(
        jnp.bfloat16
    )
    return masked.reshape(batch, frames, band_rows // 2, columns // 2 * channels)


def general_local(
    features,
    lengths,
    stored_slot,
    owner_slot,
    gain_first,
    conv_first,
    bias_first,
    gain_second,
    conv_second,
    bias_second,
    reduce_conv_weight,
    reduce_conv_bias,
):
    local_count = features.shape[0]
    my_slots = lax.axis_index("clip") * local_count + jnp.arange(local_count, dtype=jnp.int32)
    numbers = jnp.arange(stored_slot.shape[0], dtype=jnp.int32)
    placed = (stored_slot[:, None] == numbers[None, :]).astype(jnp.int32)
    target = jnp.sum(placed * owner_slot[:, None], axis=0)
    hits = (stored_slot[None, :] == my_slots[:, None]).astype(jnp.int32)
    length = jnp.sum(hits * lengths[None, :], axis=1)
    local_out = encode(
        features,
        length,
        gain_first,
        conv_first,
        bias_first,
        gain_second,
        conv_second,
        bias_second,
        reduce_conv_weight,
        reduce_conv_bias,
    )
    shard_piece = lax.all_gather(local_out, "clip", axis=0, tiled=True)
    sources = jnp.arange(shard_piece.shape[0], dtype=jnp.int32)
    source_hits = (sources[:, None] == numbers[None, :]).astype(jnp.int32)
    goes_to = jnp.sum(source_hits * target[None, :], axis=1)
    weights = (goes_to[None, :] == my_slots[:, None]).astype(shard_piece.dtype)
    return jnp.einsum(
        "ki,iabc->kabc", weights, shard_piece, preferred_element_type=jnp.float32
    ).astype(shard_piece.dtype)


CUTS = (3, 7, 11, 15)
CHUNKS = len(CUTS)


class Plan:
    def __init__(self, mesh, features, channels):
        self.blocks, self.bands, self.cores = (mesh.shape[a] for a in ("tm", "rows", "clip"))
        self.clips = features.shape[0] // self.cores
        self.frames = features.shape[1] // self.blocks
        self.band = features.shape[2] // self.bands
        self.all_frames, self.height = features.shape[1], features.shape[2]
        self.channels = channels
        self.width = features.shape[3] // channels
        self.parts = self.blocks
        self.own = self.width // self.parts
        self.window = self.own + LEFT + RIGHT
        self.pairs = self.window // 2
        self.devices = self.blocks * self.bands

    def fits(self):
        return (
            self.bands == self.clips
            and self.width % (2 * self.parts) == 0
            and 3 * (LANES - self.channels) == self.channels
            and self.band == 2
            and self.cores == 2
            and self.band * self.frames == 8
            and self.all_frames == 16
            and (self.window * self.channels) % LANES == 0
            and (self.width * self.channels) % LANES == 0
        )


def lanes_of(shape):
    return lax.broadcasted_iota(jnp.int32, shape, len(shape) - 1)


def spread_columns(plan, dense, column):
    start = column * plan.channels
    first, off = start // LANES * LANES, start % LANES
    value = dense[:, first : first + LANES]
    if off + plan.channels > LANES:
        following = dense[:, first + LANES : first + 2 * LANES]
        value = jnp.where(lanes_of(value.shape) >= off, value, following)
    if off:
        value = pltpu.roll(value, LANES - off, 1)
    return jnp.where(lanes_of(value.shape) < plan.channels, value, 0.0)


def merge_columns(plan, columns):
    rows = columns[0].shape[0]
    total = -(-len(columns) * plan.channels // LANES)
    merged = [None] * total
    for index, value in enumerate(columns):
        start = index * plan.channels
        first, off = start // LANES, start % LANES
        turned = pltpu.roll(value, off, 1) if off else value
        lane = lanes_of((rows, LANES))
        merged[first] = turned if off == 0 else jnp.where(lane >= off, turned, merged[first])
        if off + plan.channels > LANES:
            merged[first + 1] = turned
    return merged


def slot_source(plan, stored_ref, owner_ref, place):
    wanted = lax.axis_index("clip") * plan.clips + place
    source = jnp.int32(0)
    for clip in range(stored_ref.shape[0]):
        source = source + jnp.where(owner_ref[clip] == wanted, stored_ref[clip], 0)
    return source


def vectors_kernel(
    plan, lengths_ref, stored_ref, owner_ref, gain_first_ref, bias_first_ref, gain_second_ref,
    bias_second_ref, bias_reduce_ref, vector_ref,
):
    vector_ref[...] = jnp.zeros_like(vector_ref)
    for row, ref in enumerate(
        (gain_first_ref, bias_first_ref, gain_second_ref, bias_second_ref, bias_reduce_ref)
    ):
        vector_ref[row : row + 1, 0 : plan.channels] = ref[...]
    wanted = lax.axis_index("clip") * plan.clips + lax.axis_index("rows")
    length = jnp.int32(0)
    for clip in range(lengths_ref.shape[0]):
        length = length + jnp.where(owner_ref[clip] == wanted, lengths_ref[clip], 0)
    vector_ref[5:6, :] = jnp.full((1, LANES), length, jnp.int32).astype(jnp.float32)


def gather_vectors(plan, lengths, stored_slot, owner_slot, vectors):
    vmem = pl.BlockSpec(memory_space=pltpu.VMEM)
    smem = pl.BlockSpec(memory_space=pltpu.SMEM)
    return pl.pallas_call(
        functools.partial(vectors_kernel, plan),
        out_shape=jax.ShapeDtypeStruct((8, LANES), jnp.float32),
        in_specs=[smem] * 3 + [vmem] * 5,
        out_specs=vmem,
        compiler_params=pltpu.CompilerParams(vmem_limit_bytes=4 * 2**20),
    )(
        lengths,
        stored_slot,
        owner_slot,
        *(vector.reshape(1, plan.channels) for vector in vectors),
    )


def stage_kernel(source_ref, out_ref, sem):
    copy = pltpu.make_async_copy(source_ref, out_ref, sem)
    copy.start()
    copy.wait()


def stage(features):
    return pl.pallas_call(
        stage_kernel,
        out_shape=jax.ShapeDtypeStruct(features.shape, features.dtype),
        in_specs=[pl.BlockSpec(memory_space=pl.ANY)],
        out_specs=pl.BlockSpec(memory_space=pltpu.VMEM),
        scratch_shapes=[pltpu.SemaphoreType.DMA],
        compiler_params=pltpu.CompilerParams(vmem_limit_bytes=4 * 2**20),
    )(features)


def pack_kernel(plan, stored_ref, owner_ref, vector_ref, mine_ref, other_ref, out_ref, wide_ref):
    channels, frames = plan.channels, plan.frames
    lead = -(-LEFT * channels // LANES) * LANES
    inner = plan.width * channels
    ahead, count = lead // LANES, inner // LANES
    wide_ref[:, :ahead] = jnp.zeros((plan.clips, ahead, 8, LANES), jnp.float32)
    after = wide_ref.shape[1] - ahead - count
    wide_ref[:, ahead + count :] = jnp.zeros((plan.clips, after, 8, LANES), jnp.float32)
    for clip in range(plan.clips):
        source = slot_source(plan, stored_ref, owner_ref, clip)
        local = source % plan.clips
        is_mine = source // plan.clips == lax.axis_index("clip")

        def spread_frames(features_ref):
            for frame in range(frames):
                rows = features_ref[local, frame].astype(jnp.float32)
                for tile in range(count):
                    wide_ref[clip, ahead + tile, pl.ds(frame, plan.band, stride=frames), :] = rows[
                        :, tile * LANES : (tile + 1) * LANES
                    ]

        @pl.when(is_mine)
        def _():
            spread_frames(mine_ref)

        @pl.when(jnp.logical_not(is_mine))
        def _():
            spread_frames(other_ref)

        for q in range(plan.parts):
            start = lead + (q * plan.own - LEFT) * channels
            off = start % LANES
            for tile in range(plan.window * channels // LANES):
                first = start // LANES + tile
                value = wide_ref[clip, first]
                if off:
                    following = wide_ref[clip, first + 1]
                    value = jnp.where(lanes_of(value.shape) >= off, value, following)
                    value = pltpu.roll(value, LANES - off, 1)
                out_ref[clip * plan.parts + q, :, tile * LANES : (tile + 1) * LANES] = (
                    value.astype(jnp.bfloat16)
                )


def pack(plan, stored_slot, owner_slot, vectors, mine, other):
    channels = plan.channels
    lead = -(-LEFT * channels // LANES) * LANES
    total = -(-(lead + (plan.width + RIGHT) * channels) // LANES)
    vmem = pl.BlockSpec(memory_space=pltpu.VMEM)
    smem = pl.BlockSpec(memory_space=pltpu.SMEM)
    piece_rows = plan.band * plan.frames
    return pl.pallas_call(
        functools.partial(pack_kernel, plan),
        out_shape=jax.ShapeDtypeStruct(
            (plan.devices, piece_rows, plan.window * channels), jnp.bfloat16
        ),
        in_specs=[smem, smem, pl.BlockSpec(memory_space=pl.ANY), vmem, vmem],
        out_specs=vmem,
        scratch_shapes=[pltpu.VMEM((plan.clips, total, piece_rows, LANES), jnp.float32)],
        compiler_params=pltpu.CompilerParams(vmem_limit_bytes=16 * 2**20),
    )(stored_slot, owner_slot, vectors, mine, other)


def finish_kernel(plan, pieces_ref, out_ref):
    clips, channels = plan.clips, plan.channels
    used = plan.own // 2 * channels
    lane = lanes_of((plan.frames, LANES))
    for place in range(clips):
        tiles = [None] * (plan.parts * used // LANES)
        for q in range(plan.parts):
            piece = pieces_ref[place * plan.parts + q].astype(jnp.float32)
            first, off = q * used // LANES, q * used % LANES
            before = tiles[first] if off else None
            for index in range(piece.shape[1] // LANES):
                value = piece[:, index * LANES : (index + 1) * LANES]
                turned = pltpu.roll(value, off, 1) if off else value
                if first + index < len(tiles):
                    tiles[first + index] = jnp.where(lane >= off, turned, before) if off else turned
                before = turned
            if first + index + 1 < len(tiles):
                tiles[first + index + 1] = turned
        for index, value in enumerate(tiles):
            out_ref[place, :, index * LANES : (index + 1) * LANES] = value.astype(jnp.bfloat16)


def finish(plan, pieces):
    vmem = pl.BlockSpec(memory_space=pltpu.VMEM)
    width = plan.parts * (plan.own // 2) * plan.channels
    return pl.pallas_call(
        functools.partial(finish_kernel, plan),
        out_shape=jax.ShapeDtypeStruct((plan.clips, plan.frames, width), jnp.bfloat16),
        in_specs=[vmem],
        out_specs=vmem,
        compiler_params=pltpu.CompilerParams(vmem_limit_bytes=16 * 2**20),
    )(pieces)


def weight_rows():
    conv, reduction = 9 * 3 * LANES, 9 * LANES
    return conv, 2 * conv, 2 * conv + reduction


def spread_conv(plan, weight_ref, big_ref, base):
    channels = plan.channels
    spare = LANES - channels
    count = 9 * 3 * LANES
    big_ref[base : base + count] = jnp.zeros((count, 2 * LANES), big_ref.dtype)
    for tap in range(9):
        for side in range(2):
            for step in range(3):
                tile = side + step
                along = pl.ds(side * LANES, channels)
                if tile < 3:
                    first = base + (tap * 3 + tile) * LANES
                    big_ref[first : first + channels, along] = weight_ref[tap * 3 + step]
                    continue
                for tile in range(3):
                    first = base + (tap * 3 + tile) * LANES + channels
                    big_ref[first : first + spare, along] = weight_ref[
                        tap * 3 + step, tile * spare : (tile + 1) * spare
                    ]


def spread_reduction(plan, weight_ref, big_ref, base):
    big_ref[base:] = jnp.zeros_like(big_ref[base:])
    for tap in range(9):
        first = base + tap * LANES
        big_ref[first : first + plan.channels, 0 : plan.channels] = weight_ref[tap]


def encode_kernel(
    plan,
    pieces_ref,
    vector_ref,
    conv_first_ref,
    conv_second_ref,
    conv_reduce_ref,
    out_ref,
    x_ref,
    act_first_ref,
    act_second_ref,
    wide_first_ref,
    wide_second_ref,
    conv_ref,
    block_ref,
    reduced_ref,
    weights_ref,
):
    frames, height, pairs, channels = plan.all_frames, plan.height, plan.pairs, plan.channels
    rows = height * frames
    part = lax.axis_index("tm")

    conv_rows, reduce_rows, end_rows = weight_rows()
    spread_conv(plan, conv_first_ref, weights_ref, 0)
    spread_conv(plan, conv_second_ref, weights_ref, conv_rows)
    spread_reduction(plan, conv_reduce_ref, weights_ref, reduce_rows)

    half = plan.frames
    sublane = lax.broadcasted_iota(jnp.int32, (8, LANES), 0)
    for band in range(plan.bands):
        dense = [
            pieces_ref[band * plan.blocks + block].astype(jnp.float32)
            for block in range(plan.blocks)
        ]
        for column in range(plan.window):
            spread = [spread_columns(plan, piece, column) for piece in dense]
            turned = [pltpu.roll(value, half, 0) for value in spread]
            upper = [
                jnp.where(sublane < half, spread[2 * i], turned[2 * i + 1])
                for i in range(len(spread) // 2)
            ]
            lower = [
                jnp.where(sublane < half, turned[2 * i], spread[2 * i + 1])
                for i in range(len(spread) // 2)
            ]
            x_ref[column, 2 * band] = jnp.concatenate(upper, axis=0)
            x_ref[column, 2 * band + 1] = jnp.concatenate(lower, axis=0)

    def sum_matrix():
        shape = (2 * LANES, 2 * LANES)
        across = lax.broadcasted_iota(jnp.int32, shape, 0) // LANES
        along = lax.broadcasted_iota(jnp.int32, shape, 1) // LANES
        return jnp.where(across == along, 1.0, 0.0).astype(jnp.bfloat16)

    ones = sum_matrix()
    frame_of_row = lax.broadcasted_iota(jnp.int32, (rows, LANES), 0) % frames

    def in_image(pair):
        lane = lax.broadcasted_iota(jnp.int32, (1, 2 * LANES), 1)
        column = part * plan.own - LEFT + 2 * pair + lane // LANES
        return (column >= 0) & (column < plan.width)

    def activate(wide_ref, pair, values, gain):
        squares = (values * values).astype(jnp.bfloat16)
        sums = jnp.dot(squares, ones, preferred_element_type=jnp.float32)
        scale = jnp.where(in_image(pair), gain * (0.5 * channels**0.5), 0.0)
        scaled = values * lax.rsqrt(sums + channels * NORM_EPS) * scale
        wide_ref[pair + 1] = scaled + scaled * jnp.tanh(scaled)

    lane = lax.broadcasted_iota(jnp.int32, (rows, LANES), 1)

    def stack_window(wide_ref, act_ref, pair):
        before, after = wide_ref[pair, :, LANES:], wide_ref[pair + 2, :, :LANES]
        for tile, value in enumerate(
            (before, wide_ref[pair + 1, :, :LANES], wide_ref[pair + 1, :, LANES:])
        ):
            spill = pltpu.roll(after, channels - tile * (LANES - channels), 1)
            value = jnp.where(lane < channels, value, spill)
            for shift in range(3):
                moved = value
                if shift:
                    moved = jnp.where(frame_of_row >= shift, pltpu.roll(value, shift, 0), 0.0)
                act_ref[
                    2 - shift, pair, 1 : height + 1, :, tile * LANES : (tile + 1) * LANES
                ] = moved.astype(jnp.bfloat16).reshape(height, frames, LANES)

    def both(row):
        vector = vector_ref[row : row + 1, :]
        return jnp.concatenate([vector, vector], axis=1)

    first_weights = slice(0, conv_rows)
    second_weights = slice(conv_rows, reduce_rows)

    def convolve(act_ref, weights, first_pair, count):
        parts = [
            act_ref[
                tap // 3, first_pair : first_pair + count, tap % 3 : tap % 3 + height
            ].reshape(
                count * rows, 3 * LANES
            )
            for tap in range(9)
        ]
        stack = jnp.concatenate(parts, axis=1)
        return jnp.dot(stack, weights_ref[weights], preferred_element_type=jnp.float32)

    for act_ref in (act_first_ref, act_second_ref):
        act_ref[:, :, 0] = jnp.zeros_like(act_ref[:, :, 0])
        act_ref[:, :, height + 1] = jnp.zeros_like(act_ref[:, :, height + 1])
    wide_first_ref[0] = jnp.zeros_like(wide_first_ref[0])
    wide_second_ref[pairs] = jnp.zeros_like(wide_second_ref[pairs])
    block_ref[:, height] = jnp.zeros_like(block_ref[:, height])

    gain_first, gain_second = both(0), both(2)
    bias_first, bias_second = both(1), both(3)

    def first_window(acts, windows):
        for pair in acts:
            values = jnp.concatenate(
                [x_ref[2 * pair + side].reshape(rows, LANES) for side in range(2)], axis=1
            )
            activate(wide_first_ref, pair, values, gain_first)
        for pair in windows:
            stack_window(wide_first_ref, act_first_ref, pair)

    def second_window(acts, windows):
        for pair in acts:
            activate(wide_second_ref, pair, conv_ref[pair], gain_second)
        for pair in windows:
            stack_window(wide_second_ref, act_second_ref, pair)

    def first_conv(todo):
        result = convolve(act_first_ref, first_weights, todo[0], len(todo)) + bias_first
        for i, pair in enumerate(todo):
            conv_ref[pair] = result[i * rows : (i + 1) * rows]

    def second_conv(todo):
        result = convolve(act_second_ref, second_weights, todo[0], len(todo)) + bias_second
        for i, pair in enumerate(todo):
            for side in range(2):
                value = result[i * rows : (i + 1) * rows, side * LANES : (side + 1) * LANES]
                value = value.reshape(height, frames, LANES) + x_ref[2 * pair + side]
                column = part * plan.own - LEFT + 2 * pair + side
                value = jnp.where((column >= 0) & (column < plan.width), value, 0.0)
                block_ref[2 * pair + side, 0:height] = value.astype(jnp.bfloat16)

    outputs, half_rows = plan.own // 2, height // 2
    size = half_rows * frames

    def reduce_conv(todo):
        stacks = [
            jnp.concatenate(
                [
                    jnp.concatenate(
                        [
                            block_ref[LEFT + 2 * j + tap % 3, 2 * i + tap // 3]
                            for i in range(half_rows)
                        ],
                        axis=0,
                    )
                    for tap in range(9)
                ],
                axis=1,
            )
            for j in todo
        ]
        result = jnp.dot(
            jnp.concatenate(stacks, axis=0),
            weights_ref[reduce_rows:end_rows, 0:LANES],
            preferred_element_type=jnp.float32,
        )
        for i, j in enumerate(todo):
            reduced_ref[j] = result[i * size : (i + 1) * size] + vector_ref[4:5, :]

    last = pairs - 1
    cuts = [0] + [last * end // CUTS[-1] for end in CUTS]
    first_chunks = [range(a, b) for a, b in zip(cuts[:-1], cuts[1:])]
    second_cuts = [1] + [cut - 1 for cut in cuts[1:-1]] + [last]
    second_chunks = [range(a, b) for a, b in zip(second_cuts[:-1], second_cuts[1:])]
    done = 0
    reduced_until = 0
    for step in range(CHUNKS + 4):
        if 0 <= step - 1 < CHUNKS:
            first_conv(first_chunks[step - 1])
        if 0 <= step - 3 < CHUNKS and len(second_chunks[step - 3]):
            second_conv(second_chunks[step - 3])
        if 0 <= step - 4 < CHUNKS:
            until = min(second_chunks[step - 4].stop - 2, outputs)
            if until > reduced_until:
                reduce_conv(range(reduced_until, until))
                reduced_until = until
        if step < CHUNKS:
            until = first_chunks[step].stop + 1
            first_window(range(done, until), first_chunks[step])
            done = until
        if 0 <= step - 2 < CHUNKS:
            second_window(first_chunks[step - 2], second_chunks[step - 2])

    alive = lax.broadcasted_iota(jnp.int32, (size, LANES), 0) % frames
    alive = alive.astype(jnp.float32) < vector_ref[5:6, :]
    merged = merge_columns(
        plan, [jnp.where(alive, reduced_ref[j], 0.0) for j in range(outputs)]
    )
    for tile, value in enumerate(merged):
        for i in range(half_rows):
            for block in range(plan.blocks):
                first = i * frames + block * plan.frames
                out_ref[i * plan.blocks + block, :, tile * LANES : (tile + 1) * LANES] = value[
                    first : first + plan.frames
                ].astype(jnp.bfloat16)


def encode_window(plan, pieces, vectors, conv_first, conv_second, reduce_conv_weight):
    channels, pairs = plan.channels, plan.pairs
    rows = plan.height * plan.all_frames
    out_tiles = -(-plan.own // 2 * channels // LANES)
    vmem = pl.BlockSpec(memory_space=pltpu.VMEM)
    acts = pltpu.VMEM((3, pairs, plan.height + 2, plan.all_frames, 3 * LANES), jnp.bfloat16)
    wide = pltpu.VMEM((pairs + 2, rows, 2 * LANES), jnp.float32)
    return pl.pallas_call(
        functools.partial(encode_kernel, plan),
        out_shape=jax.ShapeDtypeStruct(
            (plan.devices, plan.frames, out_tiles * LANES), jnp.bfloat16
        ),
        in_specs=[vmem] * 5,
        out_specs=vmem,
        scratch_shapes=[
            pltpu.VMEM((plan.window, plan.height, plan.all_frames, LANES), jnp.float32),
            acts,
            acts,
            wide,
            wide,
            pltpu.VMEM((pairs, rows, 2 * LANES), jnp.float32),
            pltpu.VMEM((plan.window, plan.height + 1, plan.all_frames, LANES), jnp.bfloat16),
            pltpu.VMEM((plan.own // 2, rows // 2, LANES), jnp.float32),
            pltpu.VMEM((weight_rows()[2], 2 * LANES), jnp.bfloat16),
        ],
        compiler_params=pltpu.CompilerParams(vmem_limit_bytes=32 * 2**20),
    )(
        pieces,
        vectors,
        conv_first.reshape(27, channels, channels),
        conv_second.reshape(27, channels, channels),
        reduce_conv_weight.reshape(9, channels, channels),
    )


def window_local(
    plan, features, lengths, stored_slot, owner_slot, gain_first, conv_first, bias_first,
    gain_second, conv_second, bias_second, reduce_conv_weight, reduce_conv_bias,
):
    swap = [(core, plan.cores - 1 - core) for core in range(plan.cores)]
    other = lax.ppermute(features, "clip", swap)
    mine = stage(features)
    vectors = (gain_first, bias_first, gain_second, bias_second, reduce_conv_bias)
    vectors = gather_vectors(plan, lengths, stored_slot, owner_slot, vectors)
    pieces = pack(plan, stored_slot, owner_slot, vectors, mine, other)
    pieces = lax.all_to_all(pieces, ("rows", "tm"), 0, 0, tiled=True)
    out = encode_window(plan, pieces, vectors, conv_first, conv_second, reduce_conv_weight)
    out = lax.all_to_all(out, ("rows", "tm"), 0, 0, tiled=True)
    out = finish(plan, out)
    return out.reshape(plan.clips, plan.frames, 1, out.shape[2])


def solution(mesh):
    out_specs = P("clip", "tm", "rows", None)
    in_specs = (out_specs,) + (P(),) * 11

    def run(features, *others):
        plan = Plan(mesh, features, others[3].shape[0])
        inner = functools.partial(window_local, plan) if plan.fits() else general_local
        return jax.shard_map(
            inner, mesh=mesh, in_specs=in_specs, out_specs=out_specs, check_vma=False
        )(features, *others)

    return run
```

```python
import functools

import jax
import jax.numpy as jnp
from jax import lax
from jax.experimental import pallas as pl
from jax.experimental.pallas import tpu as pltpu
from jax.sharding import PartitionSpec as P

NORM_EPS = 1e-06
LANES = 128
LEFT, RIGHT = 2, 4


def from_behind(value, axis, steps):
    count = lax.axis_size(axis)
    first, last = (max(0, -steps), min(count, count - steps))
    return lax.ppermute(value, axis, [(source, source + steps) for source in range(first, last)])


def padded_2(x, sides, width):
    for axis, dim in sides:
        count, length = (lax.axis_size(axis), x.shape[dim])
        up = [(i, (i + 1) % count) for i in range(count - 1)]
        down = [(j, i) for i, j in up]
        last = lax.slice_in_dim(x, length - width, length, axis=dim)
        first = lax.slice_in_dim(x, 0, width, axis=dim)
        before = lax.ppermute(last, axis, up)
        after = lax.ppermute(first, axis, down)
        x = jnp.concatenate([before, x, after], axis=dim)
    return x


def norm_silu(values, gain_vec):
    scaled = (
        values * lax.rsqrt(jnp.mean(values * values, axis=-1, keepdims=True) + NORM_EPS) * gain_vec
    )
    return jax.nn.silu(scaled)


def conv_valid(grown_block, kernel_weight, bias_vector):
    batch = grown_block.shape[0]
    frames = grown_block.shape[1] - 2
    band_rows = grown_block.shape[2] - 2
    columns = grown_block.shape[3]
    channels = grown_block.shape[4]
    outputs = kernel_weight.shape[4]
    padded = jnp.pad(grown_block, ((0, 0), (0, 0), (0, 0), (1, 1), (0, 0)))
    running_sum = jnp.zeros((batch * frames * band_rows * columns, outputs), jnp.float32)
    for step_t in range(3):
        for step_h in range(3):
            window = padded[:, step_t : step_t + frames, step_h : step_h + band_rows]
            tap_stack = jnp.concatenate(
                [window[:, :, :, step_w : step_w + columns] for step_w in range(3)], axis=-1
            )
            running_sum = running_sum + jnp.dot(
                tap_stack.reshape(-1, 3 * channels),
                kernel_weight[step_t, step_h].reshape(3 * channels, outputs),
                preferred_element_type=jnp.float32,
            )
    return (running_sum + bias_vector).reshape(batch, frames, band_rows, columns, outputs)


def spatial_reduce(padded_frames, kernel_weight, bias_vector):
    batch = padded_frames.shape[0]
    frames = padded_frames.shape[1]
    half_rows = (padded_frames.shape[2] - 1) // 2
    columns = padded_frames.shape[3]
    channels = padded_frames.shape[4]
    outputs = kernel_weight.shape[3]
    padded = jnp.pad(padded_frames, ((0, 0), (0, 0), (0, 0), (0, 1), (0, 0)))
    running_sum = jnp.zeros((batch * frames * half_rows * (columns // 2), outputs), jnp.float32)
    for step_h in range(3):
        row_band = padded[:, :, step_h : step_h + 2 * half_rows - 1 : 2]
        tap_stack = jnp.concatenate(
            [row_band[:, :, :, step_w : step_w + columns - 1 : 2] for step_w in range(3)], axis=-1
        )
        running_sum = running_sum + jnp.dot(
            tap_stack.reshape(-1, 3 * channels),
            kernel_weight[step_h].reshape(3 * channels, outputs),
            preferred_element_type=jnp.float32,
        )
    return (running_sum + bias_vector).reshape(batch, frames, half_rows, columns // 2, outputs)


def encode(
    clip_block,
    length,
    gain_first,
    conv_first,
    bias_first,
    gain_second,
    conv_second,
    bias_second,
    reduce_conv_weight,
    reduce_conv_bias,
):
    batch = clip_block.shape[0]
    frames = clip_block.shape[1]
    band_rows = clip_block.shape[2]
    channels = gain_first.shape[0]
    columns = clip_block.shape[3] // channels
    feature_map = clip_block.reshape(batch, frames, band_rows, columns, channels)
    first_frame = lax.axis_index("tm") * frames
    first_act = norm_silu(feature_map.astype(jnp.float32), gain_first).astype(jnp.bfloat16)
    earlier = from_behind(first_act[:, frames - 2 :], "tm", 1)
    grown_block = padded_2(jnp.concatenate([earlier, first_act], axis=1), (("rows", 2),), 1)
    first_conv = conv_valid(grown_block, conv_first, bias_first)
    second_act = norm_silu(first_conv, gain_second).astype(jnp.bfloat16)
    earlier_two = from_behind(second_act[:, frames - 2 :], "tm", 1)
    grown_two = padded_2(jnp.concatenate([earlier_two, second_act], axis=1), (("rows", 2),), 1)
    branch = conv_valid(grown_two, conv_second, bias_second)
    residual_block_output = (feature_map.astype(jnp.float32) + branch).astype(jnp.bfloat16)
    lower_neighbor_row = from_behind(residual_block_output[:, :, :1], "rows", -1)
    spatial_reduced = spatial_reduce(
        jnp.concatenate([residual_block_output, lower_neighbor_row], axis=2),
        reduce_conv_weight,
        reduce_conv_bias,
    )
    alive_frame = (first_frame + jnp.arange(frames, dtype=jnp.int32))[None, :] < length[:, None]
    masked = jnp.where(alive_frame[:, :, None, None, None], spatial_reduced, 0.0).astype(
        jnp.bfloat16
    )
    return masked.reshape(batch, frames, band_rows // 2, columns // 2 * channels)


def general_local(
    features,
    lengths,
    stored_slot,
    owner_slot,
    gain_first,
    conv_first,
    bias_first,
    gain_second,
    conv_second,
    bias_second,
    reduce_conv_weight,
    reduce_conv_bias,
):
    local_count = features.shape[0]
    my_slots = lax.axis_index("clip") * local_count + jnp.arange(local_count, dtype=jnp.int32)
    numbers = jnp.arange(stored_slot.shape[0], dtype=jnp.int32)
    placed = (stored_slot[:, None] == numbers[None, :]).astype(jnp.int32)
    target = jnp.sum(placed * owner_slot[:, None], axis=0)
    hits = (stored_slot[None, :] == my_slots[:, None]).astype(jnp.int32)
    length = jnp.sum(hits * lengths[None, :], axis=1)
    local_out = encode(
        features,
        length,
        gain_first,
        conv_first,
        bias_first,
        gain_second,
        conv_second,
        bias_second,
        reduce_conv_weight,
        reduce_conv_bias,
    )
    shard_piece = lax.all_gather(local_out, "clip", axis=0, tiled=True)
    sources = jnp.arange(shard_piece.shape[0], dtype=jnp.int32)
    source_hits = (sources[:, None] == numbers[None, :]).astype(jnp.int32)
    goes_to = jnp.sum(source_hits * target[None, :], axis=1)
    weights = (goes_to[None, :] == my_slots[:, None]).astype(shard_piece.dtype)
    return jnp.einsum(
        "ki,iabc->kabc", weights, shard_piece, preferred_element_type=jnp.float32
    ).astype(shard_piece.dtype)


CUTS = (3, 7, 11, 15)
CHUNKS = len(CUTS)


class Plan:
    def __init__(self, mesh, features, channels):
        self.blocks, self.bands, self.cores = (mesh.shape[a] for a in ("tm", "rows", "clip"))
        self.clips = features.shape[0] // self.cores
        self.frames = features.shape[1] // self.blocks
        self.band = features.shape[2] // self.bands
        self.all_frames, self.height = features.shape[1], features.shape[2]
        self.channels = channels
        self.width = features.shape[3] // channels
        self.parts = self.blocks
        self.own = self.width // self.parts
        self.window = self.own + LEFT + RIGHT
        self.pairs = self.window // 2
        self.devices = self.blocks * self.bands

    def fits(self):
        return (
            self.bands == self.clips
            and self.width % (2 * self.parts) == 0
            and 3 * (LANES - self.channels) == self.channels
            and self.band == 2
            and self.cores == 2
            and self.band * self.frames == 8
            and self.all_frames == 16
            and (self.window * self.channels) % LANES == 0
            and (self.width * self.channels) % LANES == 0
        )


def lanes_of(shape):
    return lax.broadcasted_iota(jnp.int32, shape, len(shape) - 1)


def spread_columns(plan, dense, column):
    start = column * plan.channels
    first, off = start // LANES * LANES, start % LANES
    value = dense[:, first : first + LANES]
    if off + plan.channels > LANES:
        following = dense[:, first + LANES : first + 2 * LANES]
        value = jnp.where(lanes_of(value.shape) >= off, value, following)
    if off:
        value = pltpu.roll(value, LANES - off, 1)
    return jnp.where(lanes_of(value.shape) < plan.channels, value, 0.0)


def merge_columns(plan, columns):
    rows = columns[0].shape[0]
    total = -(-len(columns) * plan.channels // LANES)
    merged = [None] * total
    for index, value in enumerate(columns):
        start = index * plan.channels
        first, off = start // LANES, start % LANES
        turned = pltpu.roll(value, off, 1) if off else value
        lane = lanes_of((rows, LANES))
        merged[first] = turned if off == 0 else jnp.where(lane >= off, turned, merged[first])
        if off + plan.channels > LANES:
            merged[first + 1] = turned
    return merged


def slot_source(plan, stored_ref, owner_ref, place):
    wanted = lax.axis_index("clip") * plan.clips + place
    source = jnp.int32(0)
    for clip in range(stored_ref.shape[0]):
        source = source + jnp.where(owner_ref[clip] == wanted, stored_ref[clip], 0)
    return source


def vectors_kernel(
    plan, lengths_ref, stored_ref, owner_ref, gain_first_ref, bias_first_ref, gain_second_ref,
    bias_second_ref, bias_reduce_ref, vector_ref,
):
    vector_ref[...] = jnp.zeros_like(vector_ref)
    for row, ref in enumerate(
        (gain_first_ref, bias_first_ref, gain_second_ref, bias_second_ref, bias_reduce_ref)
    ):
        vector_ref[row : row + 1, 0 : plan.channels] = ref[...]
    wanted = lax.axis_index("clip") * plan.clips + lax.axis_index("rows")
    length = jnp.int32(0)
    for clip in range(lengths_ref.shape[0]):
        length = length + jnp.where(owner_ref[clip] == wanted, lengths_ref[clip], 0)
    vector_ref[5:6, :] = jnp.full((1, LANES), length, jnp.int32).astype(jnp.float32)


def gather_vectors(plan, lengths, stored_slot, owner_slot, vectors):
    vmem = pl.BlockSpec(memory_space=pltpu.VMEM)
    smem = pl.BlockSpec(memory_space=pltpu.SMEM)
    return pl.pallas_call(
        functools.partial(vectors_kernel, plan),
        out_shape=jax.ShapeDtypeStruct((8, LANES), jnp.float32),
        in_specs=[smem] * 3 + [vmem] * 5,
        out_specs=vmem,
        compiler_params=pltpu.CompilerParams(vmem_limit_bytes=4 * 2**20),
    )(
        lengths,
        stored_slot,
        owner_slot,
        *(vector.reshape(1, plan.channels) for vector in vectors),
    )


def stage_kernel(source_ref, out_ref, sem):
    copy = pltpu.make_async_copy(source_ref, out_ref, sem)
    copy.start()
    copy.wait()


def stage(features):
    return pl.pallas_call(
        stage_kernel,
        out_shape=jax.ShapeDtypeStruct(features.shape, features.dtype),
        in_specs=[pl.BlockSpec(memory_space=pl.ANY)],
        out_specs=pl.BlockSpec(memory_space=pltpu.VMEM),
        scratch_shapes=[pltpu.SemaphoreType.DMA],
        compiler_params=pltpu.CompilerParams(vmem_limit_bytes=4 * 2**20),
    )(features)


def pack_kernel(plan, stored_ref, owner_ref, vector_ref, mine_ref, other_ref, out_ref, wide_ref):
    channels, frames = plan.channels, plan.frames
    lead = -(-LEFT * channels // LANES) * LANES
    inner = plan.width * channels
    ahead, count = lead // LANES, inner // LANES
    wide_ref[:, :ahead] = jnp.zeros((plan.clips, ahead, 8, LANES), jnp.float32)
    after = wide_ref.shape[1] - ahead - count
    wide_ref[:, ahead + count :] = jnp.zeros((plan.clips, after, 8, LANES), jnp.float32)
    for clip in range(plan.clips):
        source = slot_source(plan, stored_ref, owner_ref, clip)
        local = source % plan.clips
        is_mine = source // plan.clips == lax.axis_index("clip")

        def spread_frames(features_ref):
            for frame in range(frames):
                rows = features_ref[local, frame].astype(jnp.float32)
                for tile in range(count):
                    wide_ref[clip, ahead + tile, pl.ds(frame, plan.band, stride=frames), :] = rows[
                        :, tile * LANES : (tile + 1) * LANES
                    ]

        @pl.when(is_mine)
        def _():
            spread_frames(mine_ref)

        @pl.when(jnp.logical_not(is_mine))
        def _():
            spread_frames(other_ref)

        for q in range(plan.parts):
            start = lead + (q * plan.own - LEFT) * channels
            off = start % LANES
            for tile in range(plan.window * channels // LANES):
                first = start // LANES + tile
                value = wide_ref[clip, first]
                if off:
                    following = wide_ref[clip, first + 1]
                    value = jnp.where(lanes_of(value.shape) >= off, value, following)
                    value = pltpu.roll(value, LANES - off, 1)
                out_ref[clip * plan.parts + q, :, tile * LANES : (tile + 1) * LANES] = (
                    value.astype(jnp.bfloat16)
                )


def pack(plan, stored_slot, owner_slot, vectors, mine, other):
    channels = plan.channels
    lead = -(-LEFT * channels // LANES) * LANES
    total = -(-(lead + (plan.width + RIGHT) * channels) // LANES)
    vmem = pl.BlockSpec(memory_space=pltpu.VMEM)
    smem = pl.BlockSpec(memory_space=pltpu.SMEM)
    piece_rows = plan.band * plan.frames
    return pl.pallas_call(
        functools.partial(pack_kernel, plan),
        out_shape=jax.ShapeDtypeStruct(
            (plan.devices, piece_rows, plan.window * channels), jnp.bfloat16
        ),
        in_specs=[smem, smem, pl.BlockSpec(memory_space=pl.ANY), vmem, vmem],
        out_specs=vmem,
        scratch_shapes=[pltpu.VMEM((plan.clips, total, piece_rows, LANES), jnp.float32)],
        compiler_params=pltpu.CompilerParams(vmem_limit_bytes=16 * 2**20),
    )(stored_slot, owner_slot, vectors, mine, other)


def finish_kernel(plan, pieces_ref, out_ref):
    clips, channels = plan.clips, plan.channels
    used = plan.own // 2 * channels
    lane = lanes_of((plan.frames, LANES))
    for place in range(clips):
        tiles = [None] * (plan.parts * used // LANES)
        for q in range(plan.parts):
            piece = pieces_ref[place * plan.parts + q].astype(jnp.float32)
            first, off = q * used // LANES, q * used % LANES
            before = tiles[first] if off else None
            for index in range(piece.shape[1] // LANES):
                value = piece[:, index * LANES : (index + 1) * LANES]
                turned = pltpu.roll(value, off, 1) if off else value
                if first + index < len(tiles):
                    tiles[first + index] = jnp.where(lane >= off, turned, before) if off else turned
                before = turned
            if first + index + 1 < len(tiles):
                tiles[first + index + 1] = turned
        for index, value in enumerate(tiles):
            out_ref[place, :, index * LANES : (index + 1) * LANES] = value.astype(jnp.bfloat16)


def finish(plan, pieces):
    vmem = pl.BlockSpec(memory_space=pltpu.VMEM)
    width = plan.parts * (plan.own // 2) * plan.channels
    return pl.pallas_call(
        functools.partial(finish_kernel, plan),
        out_shape=jax.ShapeDtypeStruct((plan.clips, plan.frames, width), jnp.bfloat16),
        in_specs=[vmem],
        out_specs=vmem,
        compiler_params=pltpu.CompilerParams(vmem_limit_bytes=16 * 2**20),
    )(pieces)


def weight_rows():
    conv, reduction = 9 * 3 * LANES, 9 * LANES
    return conv, 2 * conv, 2 * conv + reduction


def spread_conv(plan, weight_ref, big_ref, base):
    channels = plan.channels
    spare = LANES - channels
    count = 9 * 3 * LANES
    big_ref[base : base + count] = jnp.zeros((count, 2 * LANES), big_ref.dtype)
    for tap in range(9):
        for side in range(2):
            for step in range(3):
                tile = side + step
                along = pl.ds(side * LANES, channels)
                if tile < 3:
                    first = base + (tap * 3 + tile) * LANES
                    big_ref[first : first + channels, along] = weight_ref[tap * 3 + step]
                    continue
                for tile in range(3):
                    first = base + (tap * 3 + tile) * LANES + channels
                    big_ref[first : first + spare, along] = weight_ref[
                        tap * 3 + step, tile * spare : (tile + 1) * spare
                    ]


def spread_reduction(plan, weight_ref, big_ref, base):
    big_ref[base:] = jnp.zeros_like(big_ref[base:])
    for tap in range(9):
        first = base + tap * LANES
        big_ref[first : first + plan.channels, 0 : plan.channels] = weight_ref[tap]


def encode_kernel(
    plan,
    pieces_ref,
    vector_ref,
    conv_first_ref,
    conv_second_ref,
    conv_reduce_ref,
    out_ref,
    x_ref,
    act_first_ref,
    act_second_ref,
    wide_first_ref,
    wide_second_ref,
    conv_ref,
    block_ref,
    reduced_ref,
    weights_ref,
):
    frames, height, pairs, channels = plan.all_frames, plan.height, plan.pairs, plan.channels
    rows = height * frames
    part = lax.axis_index("tm")

    conv_rows, reduce_rows, end_rows = weight_rows()
    spread_conv(plan, conv_first_ref, weights_ref, 0)
    spread_conv(plan, conv_second_ref, weights_ref, conv_rows)
    spread_reduction(plan, conv_reduce_ref, weights_ref, reduce_rows)

    half = plan.frames
    sublane = lax.broadcasted_iota(jnp.int32, (8, LANES), 0)
    for band in range(plan.bands):
        dense = [
            pieces_ref[band * plan.blocks + block].astype(jnp.float32)
            for block in range(plan.blocks)
        ]
        for column in range(plan.window):
            spread = [spread_columns(plan, piece, column) for piece in dense]
            turned = [pltpu.roll(value, half, 0) for value in spread]
            upper = [
                jnp.where(sublane < half, spread[2 * i], turned[2 * i + 1])
                for i in range(len(spread) // 2)
            ]
            lower = [
                jnp.where(sublane < half, turned[2 * i], spread[2 * i + 1])
                for i in range(len(spread) // 2)
            ]
            x_ref[column, 2 * band] = jnp.concatenate(upper, axis=0)
            x_ref[column, 2 * band + 1] = jnp.concatenate(lower, axis=0)

    def sum_matrix():
        shape = (2 * LANES, 2 * LANES)
        across = lax.broadcasted_iota(jnp.int32, shape, 0) // LANES
        along = lax.broadcasted_iota(jnp.int32, shape, 1) // LANES
        return jnp.where(across == along, 1.0, 0.0).astype(jnp.bfloat16)

    ones = sum_matrix()
    row_in_tile = lax.broadcasted_iota(jnp.int32, (height, frames // 8, 8, LANES), 2)

    def in_image(pair):
        lane = lax.broadcasted_iota(jnp.int32, (1, 2 * LANES), 1)
        column = part * plan.own - LEFT + 2 * pair + lane // LANES
        return (column >= 0) & (column < plan.width)

    def activate(wide_ref, pair, values, gain):
        squares = (values * values).astype(jnp.bfloat16)
        sums = jnp.dot(squares, ones, preferred_element_type=jnp.float32)
        scale = jnp.where(in_image(pair), gain * (0.5 * channels**0.5), 0.0)
        scaled = values * lax.rsqrt(sums + channels * NORM_EPS) * scale
        wide_ref[pair + 1] = scaled + scaled * jnp.tanh(scaled)

    lane = lax.broadcasted_iota(jnp.int32, (rows, LANES), 1)

    def stack_window(wide_ref, act_ref, pair):
        before, after = wide_ref[pair, :, LANES:], wide_ref[pair + 2, :, :LANES]
        for tile, value in enumerate(
            (before, wide_ref[pair + 1, :, :LANES], wide_ref[pair + 1, :, LANES:])
        ):
            spill = pltpu.roll(after, channels - tile * (LANES - channels), 1)
            value = jnp.where(lane < channels, value, spill)
            value = value.reshape(height, frames // 8, 8, LANES)
            for shift in range(3):
                moved = value
                if shift:
                    turned = pltpu.roll(value, shift, 2)
                    ahead = jnp.concatenate(
                        [jnp.zeros_like(turned[:, :1]), turned[:, :-1]], axis=1
                    )
                    moved = jnp.where(row_in_tile >= shift, turned, ahead)
                act_ref[
                    2 - shift, pair, 1 : height + 1, :, tile * LANES : (tile + 1) * LANES
                ] = moved.astype(jnp.bfloat16).reshape(height, frames, LANES)

    def both(row):
        vector = vector_ref[row : row + 1, :]
        return jnp.concatenate([vector, vector], axis=1)

    first_weights = slice(0, conv_rows)
    second_weights = slice(conv_rows, reduce_rows)

    def convolve(act_ref, weights, first_pair, count):
        parts = [
            act_ref[
                tap // 3, first_pair : first_pair + count, tap % 3 : tap % 3 + height
            ].reshape(
                count * rows, 3 * LANES
            )
            for tap in range(9)
        ]
        stack = jnp.concatenate(parts, axis=1)
        return jnp.dot(stack, weights_ref[weights], preferred_element_type=jnp.float32)

    for act_ref in (act_first_ref, act_second_ref):
        act_ref[:, :, 0] = jnp.zeros_like(act_ref[:, :, 0])
        act_ref[:, :, height + 1] = jnp.zeros_like(act_ref[:, :, height + 1])
    wide_first_ref[0] = jnp.zeros_like(wide_first_ref[0])
    wide_second_ref[pairs] = jnp.zeros_like(wide_second_ref[pairs])
    block_ref[:, height] = jnp.zeros_like(block_ref[:, height])

    gain_first, gain_second = both(0), both(2)
    bias_first, bias_second = both(1), both(3)

    def first_window(acts, windows):
        for pair in acts:
            values = jnp.concatenate(
                [x_ref[2 * pair + side].reshape(rows, LANES) for side in range(2)], axis=1
            )
            activate(wide_first_ref, pair, values, gain_first)
        for pair in windows:
            stack_window(wide_first_ref, act_first_ref, pair)

    def second_window(acts, windows):
        for pair in acts:
            activate(wide_second_ref, pair, conv_ref[pair], gain_second)
        for pair in windows:
            stack_window(wide_second_ref, act_second_ref, pair)

    def first_conv(todo):
        result = convolve(act_first_ref, first_weights, todo[0], len(todo)) + bias_first
        for i, pair in enumerate(todo):
            conv_ref[pair] = result[i * rows : (i + 1) * rows]

    def second_conv(todo):
        result = convolve(act_second_ref, second_weights, todo[0], len(todo)) + bias_second
        for i, pair in enumerate(todo):
            for side in range(2):
                value = result[i * rows : (i + 1) * rows, side * LANES : (side + 1) * LANES]
                value = value.reshape(height, frames, LANES) + x_ref[2 * pair + side]
                column = part * plan.own - LEFT + 2 * pair + side
                value = jnp.where((column >= 0) & (column < plan.width), value, 0.0)
                block_ref[2 * pair + side, 0:height] = value.astype(jnp.bfloat16)

    outputs, half_rows = plan.own // 2, height // 2
    size = half_rows * frames

    def reduce_conv(todo):
        stacks = [
            jnp.concatenate(
                [
                    jnp.concatenate(
                        [
                            block_ref[LEFT + 2 * j + tap % 3, 2 * i + tap // 3]
                            for i in range(half_rows)
                        ],
                        axis=0,
                    )
                    for tap in range(9)
                ],
                axis=1,
            )
            for j in todo
        ]
        result = jnp.dot(
            jnp.concatenate(stacks, axis=0),
            weights_ref[reduce_rows:end_rows, 0:LANES],
            preferred_element_type=jnp.float32,
        )
        for i, j in enumerate(todo):
            reduced_ref[j] = result[i * size : (i + 1) * size] + vector_ref[4:5, :]

    last = pairs - 1
    cuts = [0] + [last * end // CUTS[-1] for end in CUTS]
    first_chunks = [range(a, b) for a, b in zip(cuts[:-1], cuts[1:])]
    second_cuts = [1] + [cut - 1 for cut in cuts[1:-1]] + [last]
    second_chunks = [range(a, b) for a, b in zip(second_cuts[:-1], second_cuts[1:])]
    done = 0
    reduced_until = 0
    for step in range(CHUNKS + 4):
        if 0 <= step - 1 < CHUNKS:
            first_conv(first_chunks[step - 1])
        if 0 <= step - 3 < CHUNKS and len(second_chunks[step - 3]):
            second_conv(second_chunks[step - 3])
        if 0 <= step - 4 < CHUNKS:
            until = min(second_chunks[step - 4].stop - 2, outputs)
            if until > reduced_until:
                reduce_conv(range(reduced_until, until))
                reduced_until = until
        if step < CHUNKS:
            until = first_chunks[step].stop + 1
            first_window(range(done, until), first_chunks[step])
            done = until
        if 0 <= step - 2 < CHUNKS:
            second_window(first_chunks[step - 2], second_chunks[step - 2])

    alive = lax.broadcasted_iota(jnp.int32, (size, LANES), 0) % frames
    alive = alive.astype(jnp.float32) < vector_ref[5:6, :]
    merged = merge_columns(
        plan, [jnp.where(alive, reduced_ref[j], 0.0) for j in range(outputs)]
    )
    for tile, value in enumerate(merged):
        for i in range(half_rows):
            for block in range(plan.blocks):
                first = i * frames + block * plan.frames
                out_ref[i * plan.blocks + block, :, tile * LANES : (tile + 1) * LANES] = value[
                    first : first + plan.frames
                ].astype(jnp.bfloat16)


def encode_window(plan, pieces, vectors, conv_first, conv_second, reduce_conv_weight):
    channels, pairs = plan.channels, plan.pairs
    rows = plan.height * plan.all_frames
    out_tiles = -(-plan.own // 2 * channels // LANES)
    vmem = pl.BlockSpec(memory_space=pltpu.VMEM)
    acts = pltpu.VMEM((3, pairs, plan.height + 2, plan.all_frames, 3 * LANES), jnp.bfloat16)
    wide = pltpu.VMEM((pairs + 2, rows, 2 * LANES), jnp.float32)
    return pl.pallas_call(
        functools.partial(encode_kernel, plan),
        out_shape=jax.ShapeDtypeStruct(
            (plan.devices, plan.frames, out_tiles * LANES), jnp.bfloat16
        ),
        in_specs=[vmem] * 5,
        out_specs=vmem,
        scratch_shapes=[
            pltpu.VMEM((plan.window, plan.height, plan.all_frames, LANES), jnp.float32),
            acts,
            acts,
            wide,
            wide,
            pltpu.VMEM((pairs, rows, 2 * LANES), jnp.float32),
            pltpu.VMEM((plan.window, plan.height + 1, plan.all_frames, LANES), jnp.bfloat16),
            pltpu.VMEM((plan.own // 2, rows // 2, LANES), jnp.float32),
            pltpu.VMEM((weight_rows()[2], 2 * LANES), jnp.bfloat16),
        ],
        compiler_params=pltpu.CompilerParams(vmem_limit_bytes=32 * 2**20),
    )(
        pieces,
        vectors,
        conv_first.reshape(27, channels, channels),
        conv_second.reshape(27, channels, channels),
        reduce_conv_weight.reshape(9, channels, channels),
    )


def window_local(
    plan, features, lengths, stored_slot, owner_slot, gain_first, conv_first, bias_first,
    gain_second, conv_second, bias_second, reduce_conv_weight, reduce_conv_bias,
):
    swap = [(core, plan.cores - 1 - core) for core in range(plan.cores)]
    other = lax.ppermute(features, "clip", swap)
    mine = stage(features)
    vectors = (gain_first, bias_first, gain_second, bias_second, reduce_conv_bias)
    vectors = gather_vectors(plan, lengths, stored_slot, owner_slot, vectors)
    pieces = pack(plan, stored_slot, owner_slot, vectors, mine, other)
    pieces = lax.all_to_all(pieces, ("rows", "tm"), 0, 0, tiled=True)
    out = encode_window(plan, pieces, vectors, conv_first, conv_second, reduce_conv_weight)
    out = lax.all_to_all(out, ("rows", "tm"), 0, 0, tiled=True)
    out = finish(plan, out)
    return out.reshape(plan.clips, plan.frames, 1, out.shape[2])


def solution(mesh):
    out_specs = P("clip", "tm", "rows", None)
    in_specs = (out_specs,) + (P(),) * 11

    def run(features, *others):
        plan = Plan(mesh, features, others[3].shape[0])
        inner = functools.partial(window_local, plan) if plan.fits() else general_local
        return jax.shard_map(
            inner, mesh=mesh, in_specs=in_specs, out_specs=out_specs, check_vma=False
        )(features, *others)

    return run
```

```python
import functools

import jax
import jax.numpy as jnp
from jax import lax
from jax.experimental import pallas as pl
from jax.experimental.pallas import tpu as pltpu
from jax.sharding import PartitionSpec as P

NORM_EPS = 1e-06
LANES = 128
LEFT, RIGHT = 2, 4


def from_behind(value, axis, steps):
    count = lax.axis_size(axis)
    first, last = (max(0, -steps), min(count, count - steps))
    return lax.ppermute(value, axis, [(source, source + steps) for source in range(first, last)])


def padded_2(x, sides, width):
    for axis, dim in sides:
        count, length = (lax.axis_size(axis), x.shape[dim])
        up = [(i, (i + 1) % count) for i in range(count - 1)]
        down = [(j, i) for i, j in up]
        last = lax.slice_in_dim(x, length - width, length, axis=dim)
        first = lax.slice_in_dim(x, 0, width, axis=dim)
        before = lax.ppermute(last, axis, up)
        after = lax.ppermute(first, axis, down)
        x = jnp.concatenate([before, x, after], axis=dim)
    return x


def norm_silu(values, gain_vec):
    scaled = (
        values * lax.rsqrt(jnp.mean(values * values, axis=-1, keepdims=True) + NORM_EPS) * gain_vec
    )
    return jax.nn.silu(scaled)


def conv_valid(grown_block, kernel_weight, bias_vector):
    batch = grown_block.shape[0]
    frames = grown_block.shape[1] - 2
    band_rows = grown_block.shape[2] - 2
    columns = grown_block.shape[3]
    channels = grown_block.shape[4]
    outputs = kernel_weight.shape[4]
    padded = jnp.pad(grown_block, ((0, 0), (0, 0), (0, 0), (1, 1), (0, 0)))
    running_sum = jnp.zeros((batch * frames * band_rows * columns, outputs), jnp.float32)
    for step_t in range(3):
        for step_h in range(3):
            window = padded[:, step_t : step_t + frames, step_h : step_h + band_rows]
            tap_stack = jnp.concatenate(
                [window[:, :, :, step_w : step_w + columns] for step_w in range(3)], axis=-1
            )
            running_sum = running_sum + jnp.dot(
                tap_stack.reshape(-1, 3 * channels),
                kernel_weight[step_t, step_h].reshape(3 * channels, outputs),
                preferred_element_type=jnp.float32,
            )
    return (running_sum + bias_vector).reshape(batch, frames, band_rows, columns, outputs)


def spatial_reduce(padded_frames, kernel_weight, bias_vector):
    batch = padded_frames.shape[0]
    frames = padded_frames.shape[1]
    half_rows = (padded_frames.shape[2] - 1) // 2
    columns = padded_frames.shape[3]
    channels = padded_frames.shape[4]
    outputs = kernel_weight.shape[3]
    padded = jnp.pad(padded_frames, ((0, 0), (0, 0), (0, 0), (0, 1), (0, 0)))
    running_sum = jnp.zeros((batch * frames * half_rows * (columns // 2), outputs), jnp.float32)
    for step_h in range(3):
        row_band = padded[:, :, step_h : step_h + 2 * half_rows - 1 : 2]
        tap_stack = jnp.concatenate(
            [row_band[:, :, :, step_w : step_w + columns - 1 : 2] for step_w in range(3)], axis=-1
        )
        running_sum = running_sum + jnp.dot(
            tap_stack.reshape(-1, 3 * channels),
            kernel_weight[step_h].reshape(3 * channels, outputs),
            preferred_element_type=jnp.float32,
        )
    return (running_sum + bias_vector).reshape(batch, frames, half_rows, columns // 2, outputs)


def encode(
    clip_block,
    length,
    gain_first,
    conv_first,
    bias_first,
    gain_second,
    conv_second,
    bias_second,
    reduce_conv_weight,
    reduce_conv_bias,
):
    batch = clip_block.shape[0]
    frames = clip_block.shape[1]
    band_rows = clip_block.shape[2]
    channels = gain_first.shape[0]
    columns = clip_block.shape[3] // channels
    feature_map = clip_block.reshape(batch, frames, band_rows, columns, channels)
    first_frame = lax.axis_index("tm") * frames
    first_act = norm_silu(feature_map.astype(jnp.float32), gain_first).astype(jnp.bfloat16)
    earlier = from_behind(first_act[:, frames - 2 :], "tm", 1)
    grown_block = padded_2(jnp.concatenate([earlier, first_act], axis=1), (("rows", 2),), 1)
    first_conv = conv_valid(grown_block, conv_first, bias_first)
    second_act = norm_silu(first_conv, gain_second).astype(jnp.bfloat16)
    earlier_two = from_behind(second_act[:, frames - 2 :], "tm", 1)
    grown_two = padded_2(jnp.concatenate([earlier_two, second_act], axis=1), (("rows", 2),), 1)
    branch = conv_valid(grown_two, conv_second, bias_second)
    residual_block_output = (feature_map.astype(jnp.float32) + branch).astype(jnp.bfloat16)
    lower_neighbor_row = from_behind(residual_block_output[:, :, :1], "rows", -1)
    spatial_reduced = spatial_reduce(
        jnp.concatenate([residual_block_output, lower_neighbor_row], axis=2),
        reduce_conv_weight,
        reduce_conv_bias,
    )
    alive_frame = (first_frame + jnp.arange(frames, dtype=jnp.int32))[None, :] < length[:, None]
    masked = jnp.where(alive_frame[:, :, None, None, None], spatial_reduced, 0.0).astype(
        jnp.bfloat16
    )
    return masked.reshape(batch, frames, band_rows // 2, columns // 2 * channels)


def general_local(
    features,
    lengths,
    stored_slot,
    owner_slot,
    gain_first,
    conv_first,
    bias_first,
    gain_second,
    conv_second,
    bias_second,
    reduce_conv_weight,
    reduce_conv_bias,
):
    local_count = features.shape[0]
    my_slots = lax.axis_index("clip") * local_count + jnp.arange(local_count, dtype=jnp.int32)
    numbers = jnp.arange(stored_slot.shape[0], dtype=jnp.int32)
    placed = (stored_slot[:, None] == numbers[None, :]).astype(jnp.int32)
    target = jnp.sum(placed * owner_slot[:, None], axis=0)
    hits = (stored_slot[None, :] == my_slots[:, None]).astype(jnp.int32)
    length = jnp.sum(hits * lengths[None, :], axis=1)
    local_out = encode(
        features,
        length,
        gain_first,
        conv_first,
        bias_first,
        gain_second,
        conv_second,
        bias_second,
        reduce_conv_weight,
        reduce_conv_bias,
    )
    shard_piece = lax.all_gather(local_out, "clip", axis=0, tiled=True)
    sources = jnp.arange(shard_piece.shape[0], dtype=jnp.int32)
    source_hits = (sources[:, None] == numbers[None, :]).astype(jnp.int32)
    goes_to = jnp.sum(source_hits * target[None, :], axis=1)
    weights = (goes_to[None, :] == my_slots[:, None]).astype(shard_piece.dtype)
    return jnp.einsum(
        "ki,iabc->kabc", weights, shard_piece, preferred_element_type=jnp.float32
    ).astype(shard_piece.dtype)


CUTS = (3, 7, 11, 15)
CHUNKS = len(CUTS)


class Plan:
    def __init__(self, mesh, features, channels):
        self.blocks, self.bands, self.cores = (mesh.shape[a] for a in ("tm", "rows", "clip"))
        self.clips = features.shape[0] // self.cores
        self.frames = features.shape[1] // self.blocks
        self.band = features.shape[2] // self.bands
        self.all_frames, self.height = features.shape[1], features.shape[2]
        self.channels = channels
        self.width = features.shape[3] // channels
        self.parts = self.blocks
        self.own = self.width // self.parts
        self.window = self.own + LEFT + RIGHT
        self.pairs = self.window // 2
        self.devices = self.blocks * self.bands

    def fits(self):
        return (
            self.bands == self.clips
            and self.width % (2 * self.parts) == 0
            and 3 * (LANES - self.channels) == self.channels
            and self.band == 2
            and self.cores == 2
            and self.band * self.frames == 8
            and self.all_frames == 16
            and (self.window * self.channels) % LANES == 0
            and (self.width * self.channels) % LANES == 0
        )


def lanes_of(shape):
    return lax.broadcasted_iota(jnp.int32, shape, len(shape) - 1)


def spread_columns(plan, dense, column):
    start = column * plan.channels
    first, off = start // LANES * LANES, start % LANES
    value = dense[:, first : first + LANES]
    if off + plan.channels > LANES:
        following = dense[:, first + LANES : first + 2 * LANES]
        value = jnp.where(lanes_of(value.shape) >= off, value, following)
    if off:
        value = pltpu.roll(value, LANES - off, 1)
    return jnp.where(lanes_of(value.shape) < plan.channels, value, 0.0)


def merge_columns(plan, columns):
    rows = columns[0].shape[0]
    total = -(-len(columns) * plan.channels // LANES)
    merged = [None] * total
    for index, value in enumerate(columns):
        start = index * plan.channels
        first, off = start // LANES, start % LANES
        turned = pltpu.roll(value, off, 1) if off else value
        lane = lanes_of((rows, LANES))
        merged[first] = turned if off == 0 else jnp.where(lane >= off, turned, merged[first])
        if off + plan.channels > LANES:
            merged[first + 1] = turned
    return merged


def slot_source(plan, stored_ref, owner_ref, place):
    wanted = lax.axis_index("clip") * plan.clips + place
    source = jnp.int32(0)
    for clip in range(stored_ref.shape[0]):
        source = source + jnp.where(owner_ref[clip] == wanted, stored_ref[clip], 0)
    return source


def vectors_kernel(
    plan, lengths_ref, stored_ref, owner_ref, gain_first_ref, bias_first_ref, gain_second_ref,
    bias_second_ref, bias_reduce_ref, vector_ref,
):
    vector_ref[...] = jnp.zeros_like(vector_ref)
    for row, ref in enumerate(
        (gain_first_ref, bias_first_ref, gain_second_ref, bias_second_ref, bias_reduce_ref)
    ):
        vector_ref[row : row + 1, 0 : plan.channels] = ref[...]
    wanted = lax.axis_index("clip") * plan.clips + lax.axis_index("rows")
    length = jnp.int32(0)
    for clip in range(lengths_ref.shape[0]):
        length = length + jnp.where(owner_ref[clip] == wanted, lengths_ref[clip], 0)
    vector_ref[5:6, :] = jnp.full((1, LANES), length, jnp.int32).astype(jnp.float32)


def gather_vectors(plan, lengths, stored_slot, owner_slot, vectors):
    vmem = pl.BlockSpec(memory_space=pltpu.VMEM)
    smem = pl.BlockSpec(memory_space=pltpu.SMEM)
    return pl.pallas_call(
        functools.partial(vectors_kernel, plan),
        out_shape=jax.ShapeDtypeStruct((8, LANES), jnp.float32),
        in_specs=[smem] * 3 + [vmem] * 5,
        out_specs=vmem,
        compiler_params=pltpu.CompilerParams(vmem_limit_bytes=4 * 2**20),
    )(
        lengths,
        stored_slot,
        owner_slot,
        *(vector.reshape(1, plan.channels) for vector in vectors),
    )


def stage_kernel(source_ref, out_ref, sem):
    copy = pltpu.make_async_copy(source_ref, out_ref, sem)
    copy.start()
    copy.wait()


def stage(features):
    return pl.pallas_call(
        stage_kernel,
        out_shape=jax.ShapeDtypeStruct(features.shape, features.dtype),
        in_specs=[pl.BlockSpec(memory_space=pl.ANY)],
        out_specs=pl.BlockSpec(memory_space=pltpu.VMEM),
        scratch_shapes=[pltpu.SemaphoreType.DMA],
        compiler_params=pltpu.CompilerParams(vmem_limit_bytes=4 * 2**20),
    )(features)


def pack_kernel(plan, stored_ref, owner_ref, vector_ref, mine_ref, other_ref, out_ref, wide_ref):
    channels, frames = plan.channels, plan.frames
    lead = -(-LEFT * channels // LANES) * LANES
    inner = plan.width * channels
    ahead, count = lead // LANES, inner // LANES
    wide_ref[:, :ahead] = jnp.zeros((plan.clips, ahead, 8, LANES), jnp.float32)
    after = wide_ref.shape[1] - ahead - count
    wide_ref[:, ahead + count :] = jnp.zeros((plan.clips, after, 8, LANES), jnp.float32)
    for clip in range(plan.clips):
        source = slot_source(plan, stored_ref, owner_ref, clip)
        local = source % plan.clips
        is_mine = source // plan.clips == lax.axis_index("clip")

        def spread_frames(features_ref):
            for frame in range(frames):
                rows = features_ref[local, frame].astype(jnp.float32)
                for tile in range(count):
                    wide_ref[clip, ahead + tile, pl.ds(frame, plan.band, stride=frames), :] = rows[
                        :, tile * LANES : (tile + 1) * LANES
                    ]

        @pl.when(is_mine)
        def _():
            spread_frames(mine_ref)

        @pl.when(jnp.logical_not(is_mine))
        def _():
            spread_frames(other_ref)

        for q in range(plan.parts):
            start = lead + (q * plan.own - LEFT) * channels
            off = start % LANES
            for tile in range(plan.window * channels // LANES):
                first = start // LANES + tile
                value = wide_ref[clip, first]
                if off:
                    following = wide_ref[clip, first + 1]
                    value = jnp.where(lanes_of(value.shape) >= off, value, following)
                    value = pltpu.roll(value, LANES - off, 1)
                out_ref[clip * plan.parts + q, :, tile * LANES : (tile + 1) * LANES] = (
                    value.astype(jnp.bfloat16)
                )


def pack(plan, stored_slot, owner_slot, vectors, mine, other):
    channels = plan.channels
    lead = -(-LEFT * channels // LANES) * LANES
    total = -(-(lead + (plan.width + RIGHT) * channels) // LANES)
    vmem = pl.BlockSpec(memory_space=pltpu.VMEM)
    smem = pl.BlockSpec(memory_space=pltpu.SMEM)
    piece_rows = plan.band * plan.frames
    return pl.pallas_call(
        functools.partial(pack_kernel, plan),
        out_shape=jax.ShapeDtypeStruct(
            (plan.devices, piece_rows, plan.window * channels), jnp.bfloat16
        ),
        in_specs=[smem, smem, pl.BlockSpec(memory_space=pl.ANY), vmem, vmem],
        out_specs=vmem,
        scratch_shapes=[pltpu.VMEM((plan.clips, total, piece_rows, LANES), jnp.float32)],
        compiler_params=pltpu.CompilerParams(vmem_limit_bytes=16 * 2**20),
    )(stored_slot, owner_slot, vectors, mine, other)


def finish_kernel(plan, pieces_ref, out_ref):
    clips, channels = plan.clips, plan.channels
    used = plan.own // 2 * channels
    lane = lanes_of((plan.frames, LANES))
    for place in range(clips):
        tiles = [None] * (plan.parts * used // LANES)
        for q in range(plan.parts):
            piece = pieces_ref[place * plan.parts + q].astype(jnp.float32)
            first, off = q * used // LANES, q * used % LANES
            before = tiles[first] if off else None
            for index in range(piece.shape[1] // LANES):
                value = piece[:, index * LANES : (index + 1) * LANES]
                turned = pltpu.roll(value, off, 1) if off else value
                if first + index < len(tiles):
                    tiles[first + index] = jnp.where(lane >= off, turned, before) if off else turned
                before = turned
            if first + index + 1 < len(tiles):
                tiles[first + index + 1] = turned
        for index, value in enumerate(tiles):
            out_ref[place, :, index * LANES : (index + 1) * LANES] = value.astype(jnp.bfloat16)


def finish(plan, pieces):
    vmem = pl.BlockSpec(memory_space=pltpu.VMEM)
    width = plan.parts * (plan.own // 2) * plan.channels
    return pl.pallas_call(
        functools.partial(finish_kernel, plan),
        out_shape=jax.ShapeDtypeStruct((plan.clips, plan.frames, width), jnp.bfloat16),
        in_specs=[vmem],
        out_specs=vmem,
        compiler_params=pltpu.CompilerParams(vmem_limit_bytes=16 * 2**20),
    )(pieces)


def weight_rows():
    conv, reduction = 9 * 3 * LANES, 9 * LANES
    return conv, 2 * conv, 2 * conv + reduction


def spread_conv(plan, weight_ref, big_ref, base):
    channels = plan.channels
    spare = LANES - channels
    count = 9 * 3 * LANES
    big_ref[base : base + count] = jnp.zeros((count, 2 * LANES), big_ref.dtype)
    for tap in range(9):
        for side in range(2):
            for step in range(3):
                tile = side + step
                along = pl.ds(side * LANES, channels)
                if tile < 3:
                    first = base + (tap * 3 + tile) * LANES
                    big_ref[first : first + channels, along] = weight_ref[tap * 3 + step]
                    continue
                for tile in range(3):
                    first = base + (tap * 3 + tile) * LANES + channels
                    big_ref[first : first + spare, along] = weight_ref[
                        tap * 3 + step, tile * spare : (tile + 1) * spare
                    ]


def spread_reduction(plan, weight_ref, big_ref, base):
    big_ref[base:] = jnp.zeros_like(big_ref[base:])
    for tap in range(9):
        first = base + tap * LANES
        big_ref[first : first + plan.channels, 0 : plan.channels] = weight_ref[tap]


def encode_kernel(
    plan,
    pieces_ref,
    vector_ref,
    conv_first_ref,
    conv_second_ref,
    conv_reduce_ref,
    out_ref,
    x_ref,
    act_first_ref,
    act_second_ref,
    wide_first_ref,
    wide_second_ref,
    conv_ref,
    block_ref,
    reduced_ref,
    weights_ref,
):
    frames, height, pairs, channels = plan.all_frames, plan.height, plan.pairs, plan.channels
    rows = height * frames
    part = lax.axis_index("tm")

    conv_rows, reduce_rows, end_rows = weight_rows()
    spread_conv(plan, conv_first_ref, weights_ref, 0)
    spread_conv(plan, conv_second_ref, weights_ref, conv_rows)
    spread_reduction(plan, conv_reduce_ref, weights_ref, reduce_rows)

    half = plan.frames
    sublane = lax.broadcasted_iota(jnp.int32, (8, LANES), 0)
    for band in range(plan.bands):
        dense = [
            pieces_ref[band * plan.blocks + block].astype(jnp.float32)
            for block in range(plan.blocks)
        ]
        for column in range(plan.window):
            spread = [spread_columns(plan, piece, column) for piece in dense]
            turned = [pltpu.roll(value, half, 0) for value in spread]
            upper = [
                jnp.where(sublane < half, spread[2 * i], turned[2 * i + 1])
                for i in range(len(spread) // 2)
            ]
            lower = [
                jnp.where(sublane < half, turned[2 * i], spread[2 * i + 1])
                for i in range(len(spread) // 2)
            ]
            x_ref[column, 2 * band] = jnp.concatenate(upper, axis=0)
            x_ref[column, 2 * band + 1] = jnp.concatenate(lower, axis=0)

    def sum_matrix():
        shape = (2 * LANES, 2 * LANES)
        across = lax.broadcasted_iota(jnp.int32, shape, 0) // LANES
        along = lax.broadcasted_iota(jnp.int32, shape, 1) // LANES
        return jnp.where(across == along, 1.0, 0.0).astype(jnp.bfloat16)

    ones = sum_matrix()
    row_in_tile = lax.broadcasted_iota(jnp.int32, (height, frames // 8, 8, LANES), 2)

    def in_image(pair):
        lane = lax.broadcasted_iota(jnp.int32, (1, 2 * LANES), 1)
        column = part * plan.own - LEFT + 2 * pair + lane // LANES
        return (column >= 0) & (column < plan.width)

    def activate(wide_ref, pair, values, gain):
        squares = (values * values).astype(jnp.bfloat16)
        sums = jnp.dot(squares, ones, preferred_element_type=jnp.float32)
        scale = jnp.where(in_image(pair), gain * (0.5 * channels**0.5), 0.0)
        scaled = values * lax.rsqrt(sums + channels * NORM_EPS) * scale
        wide_ref[pair + 1] = scaled + scaled * jnp.tanh(scaled)

    lane = lax.broadcasted_iota(jnp.int32, (rows, LANES), 1)

    def stack_window(wide_ref, act_ref, pair):
        before, after = wide_ref[pair, :, LANES:], wide_ref[pair + 2, :, :LANES]
        for tile, value in enumerate(
            (before, wide_ref[pair + 1, :, :LANES], wide_ref[pair + 1, :, LANES:])
        ):
            spill = pltpu.roll(after, channels - tile * (LANES - channels), 1)
            value = jnp.where(lane < channels, value, spill)
            value = value.reshape(height, frames // 8, 8, LANES)
            for shift in range(3):
                moved = value
                if shift:
                    turned = pltpu.roll(value, shift, 2)
                    ahead = jnp.concatenate(
                        [jnp.zeros_like(turned[:, :1]), turned[:, :-1]], axis=1
                    )
                    moved = jnp.where(row_in_tile >= shift, turned, ahead)
                act_ref[
                    2 - shift, pair, 0:height, :, tile * LANES : (tile + 1) * LANES
                ] = moved.astype(jnp.bfloat16).reshape(height, frames, LANES)

    def both(row):
        vector = vector_ref[row : row + 1, :]
        return jnp.concatenate([vector, vector], axis=1)

    first_weights = slice(0, conv_rows)
    second_weights = slice(conv_rows, reduce_rows)

    def convolve(act_ref, weights, first_pair, count):
        parts = []
        for tap in range(9):
            chosen = act_ref.at[tap // 3, first_pair : first_pair + count]
            if tap % 3 == 0:
                window = jnp.concatenate(
                    [chosen[:, height : height + 1], chosen[:, 0 : height - 1]], axis=1
                )
            else:
                window = chosen[:, tap % 3 - 1 : tap % 3 - 1 + height]
            parts.append(window.reshape(count * rows, 3 * LANES))
        stack = jnp.concatenate(parts, axis=1)
        return jnp.dot(stack, weights_ref[weights], preferred_element_type=jnp.float32)

    for act_ref in (act_first_ref, act_second_ref):
        act_ref[:, :, height] = jnp.zeros_like(act_ref[:, :, height])
    wide_first_ref[0] = jnp.zeros_like(wide_first_ref[0])
    wide_second_ref[pairs] = jnp.zeros_like(wide_second_ref[pairs])
    block_ref[:, height] = jnp.zeros_like(block_ref[:, height])

    gain_first, gain_second = both(0), both(2)
    bias_first, bias_second = both(1), both(3)

    def first_window(acts, windows):
        for pair in acts:
            values = jnp.concatenate(
                [x_ref[2 * pair + side].reshape(rows, LANES) for side in range(2)], axis=1
            )
            activate(wide_first_ref, pair, values, gain_first)
        for pair in windows:
            stack_window(wide_first_ref, act_first_ref, pair)

    def second_window(acts, windows):
        for pair in acts:
            activate(wide_second_ref, pair, conv_ref[pair], gain_second)
        for pair in windows:
            stack_window(wide_second_ref, act_second_ref, pair)

    def first_conv(todo):
        result = convolve(act_first_ref, first_weights, todo[0], len(todo)) + bias_first
        for i, pair in enumerate(todo):
            conv_ref[pair] = result[i * rows : (i + 1) * rows]

    def second_conv(todo):
        result = convolve(act_second_ref, second_weights, todo[0], len(todo)) + bias_second
        for i, pair in enumerate(todo):
            for side in range(2):
                value = result[i * rows : (i + 1) * rows, side * LANES : (side + 1) * LANES]
                value = value.reshape(height, frames, LANES) + x_ref[2 * pair + side]
                column = part * plan.own - LEFT + 2 * pair + side
                value = jnp.where((column >= 0) & (column < plan.width), value, 0.0)
                block_ref[2 * pair + side, 0:height] = value.astype(jnp.bfloat16)

    outputs, half_rows = plan.own // 2, height // 2
    size = half_rows * frames

    def reduce_conv(todo):
        stacks = [
            jnp.concatenate(
                [
                    jnp.concatenate(
                        [
                            block_ref[LEFT + 2 * j + tap % 3, 2 * i + tap // 3]
                            for i in range(half_rows)
                        ],
                        axis=0,
                    )
                    for tap in range(9)
                ],
                axis=1,
            )
            for j in todo
        ]
        result = jnp.dot(
            jnp.concatenate(stacks, axis=0),
            weights_ref[reduce_rows:end_rows, 0:LANES],
            preferred_element_type=jnp.float32,
        )
        for i, j in enumerate(todo):
            reduced_ref[j] = result[i * size : (i + 1) * size] + vector_ref[4:5, :]

    last = pairs - 1
    cuts = [0] + [last * end // CUTS[-1] for end in CUTS]
    first_chunks = [range(a, b) for a, b in zip(cuts[:-1], cuts[1:])]
    second_cuts = [1] + [cut - 1 for cut in cuts[1:-1]] + [last]
    second_chunks = [range(a, b) for a, b in zip(second_cuts[:-1], second_cuts[1:])]
    done = 0
    reduced_until = 0
    for step in range(CHUNKS + 4):
        if 0 <= step - 1 < CHUNKS:
            first_conv(first_chunks[step - 1])
        if 0 <= step - 3 < CHUNKS and len(second_chunks[step - 3]):
            second_conv(second_chunks[step - 3])
        if 0 <= step - 4 < CHUNKS:
            until = min(second_chunks[step - 4].stop - 2, outputs)
            if until > reduced_until:
                reduce_conv(range(reduced_until, until))
                reduced_until = until
        if step < CHUNKS:
            until = first_chunks[step].stop + 1
            first_window(range(done, until), first_chunks[step])
            done = until
        if 0 <= step - 2 < CHUNKS:
            second_window(first_chunks[step - 2], second_chunks[step - 2])

    alive = lax.broadcasted_iota(jnp.int32, (size, LANES), 0) % frames
    alive = alive.astype(jnp.float32) < vector_ref[5:6, :]
    merged = merge_columns(
        plan, [jnp.where(alive, reduced_ref[j], 0.0) for j in range(outputs)]
    )
    for tile, value in enumerate(merged):
        for i in range(half_rows):
            for block in range(plan.blocks):
                first = i * frames + block * plan.frames
                out_ref[i * plan.blocks + block, :, tile * LANES : (tile + 1) * LANES] = value[
                    first : first + plan.frames
                ].astype(jnp.bfloat16)


def encode_window(plan, pieces, vectors, conv_first, conv_second, reduce_conv_weight):
    channels, pairs = plan.channels, plan.pairs
    rows = plan.height * plan.all_frames
    out_tiles = -(-plan.own // 2 * channels // LANES)
    vmem = pl.BlockSpec(memory_space=pltpu.VMEM)
    acts = pltpu.VMEM((3, pairs, plan.height + 1, plan.all_frames, 3 * LANES), jnp.bfloat16)
    wide = pltpu.VMEM((pairs + 2, rows, 2 * LANES), jnp.float32)
    return pl.pallas_call(
        functools.partial(encode_kernel, plan),
        out_shape=jax.ShapeDtypeStruct(
            (plan.devices, plan.frames, out_tiles * LANES), jnp.bfloat16
        ),
        in_specs=[vmem] * 5,
        out_specs=vmem,
        scratch_shapes=[
            pltpu.VMEM((plan.window, plan.height, plan.all_frames, LANES), jnp.float32),
            acts,
            acts,
            wide,
            wide,
            pltpu.VMEM((pairs, rows, 2 * LANES), jnp.float32),
            pltpu.VMEM((plan.window, plan.height + 1, plan.all_frames, LANES), jnp.bfloat16),
            pltpu.VMEM((plan.own // 2, rows // 2, LANES), jnp.float32),
            pltpu.VMEM((weight_rows()[2], 2 * LANES), jnp.bfloat16),
        ],
        compiler_params=pltpu.CompilerParams(vmem_limit_bytes=32 * 2**20),
    )(
        pieces,
        vectors,
        conv_first.reshape(27, channels, channels),
        conv_second.reshape(27, channels, channels),
        reduce_conv_weight.reshape(9, channels, channels),
    )


def window_local(
    plan, features, lengths, stored_slot, owner_slot, gain_first, conv_first, bias_first,
    gain_second, conv_second, bias_second, reduce_conv_weight, reduce_conv_bias,
):
    swap = [(core, plan.cores - 1 - core) for core in range(plan.cores)]
    other = lax.ppermute(features, "clip", swap)
    mine = stage(features)
    vectors = (gain_first, bias_first, gain_second, bias_second, reduce_conv_bias)
    vectors = gather_vectors(plan, lengths, stored_slot, owner_slot, vectors)
    pieces = pack(plan, stored_slot, owner_slot, vectors, mine, other)
    pieces = lax.all_to_all(pieces, ("rows", "tm"), 0, 0, tiled=True)
    out = encode_window(plan, pieces, vectors, conv_first, conv_second, reduce_conv_weight)
    out = lax.all_to_all(out, ("rows", "tm"), 0, 0, tiled=True)
    out = finish(plan, out)
    return out.reshape(plan.clips, plan.frames, 1, out.shape[2])


def solution(mesh):
    out_specs = P("clip", "tm", "rows", None)
    in_specs = (out_specs,) + (P(),) * 11

    def run(features, *others):
        plan = Plan(mesh, features, others[3].shape[0])
        inner = functools.partial(window_local, plan) if plan.fits() else general_local
        return jax.shard_map(
            inner, mesh=mesh, in_specs=in_specs, out_specs=out_specs, check_vma=False
        )(features, *others)

    return run
```
